32 devices in a mesh: blk: 4 (over y, core), dom: 8 (over z, x).
Axes of the slice: x: 2, y: 2, z: 4, core: 2. Of those that a mesh axis runs over, the one named last changes fastest.
Arguments:
- features: bfloat16 [8, 2048, 256], P('dom', 'blk'), may hold values from -6 to 6
- weight: bfloat16 [256, 256], replicated, may hold values from -0.375 to 0.375
- tiles: bfloat16 [8, 4, 4, 6, 128, 128], P('dom', 'blk'), may hold values from -0.3046875 to 0.3046875
- tile_pos: int32 [8, 4, 4, 6], P('dom', 'blk'), may hold values from 0 to 15, as said below
- tile_count: int32 [8, 4, 4], P('dom', 'blk'), may hold values from 1 to 6
- send_list: int32 [8, 4, 8, 32], P('dom', 'blk'), may hold values from 0 to 511
- send_count: int32 [8, 4, 8], P('dom', 'blk'), may hold values from 0 to 32, as said below
- owner_map: int32 [8, 4, 8, 32], P('dom', 'blk'), may hold values from 0 to 511
- halo_weight: float32 [8, 4, 8, 32], P('dom', 'blk'), may hold values from 0.25 to 1
- cotangent: bfloat16 [8, 2048, 256], P('dom', 'blk'), may hold values from -6 to 6
Outputs:
- layer_out: bfloat16 [8, 2048, 256], P('dom', 'blk')
- feature_grad: bfloat16 [8, 2048, 256], P('dom', 'blk')
- weight_grad: float32 [256, 256], replicated
The draws below stay inside these ranges and needn't reach their ends.
Inputs may be any that keep to these rules, and one draw needn't show every extreme that they name: `tile_pos`: the 6 positions of one row group in one column group are distinct. `send_count`: zero where the peer is the sender's own partition.
All inputs are finite; a program needn't handle non-finite values.
Results may differ from the reference program's by a relative error of at most 0.019.
Values may be sent and summed in bfloat16 or wider, within the bound.
No kernel may reach another device: no remote copies, remote signals or barrier semaphores. Data moves between devices by JAX's collectives and lax.ppermute only.
A program may use at most 128 MiB of HBM per device.

```python
import math
import jax
import jax.numpy as jnp
from jax import lax

F = 256
TILE = 128
ROWS = 512
SLOTS = 32
TPG = 6
VERTS = 2048
N_BLK = 4
N_DOM = 8


def draw_tile_pos(key, part):
    count = (ROWS // TILE) ** 2
    scores = jax.random.randint(key, (N_DOM, N_BLK, N_BLK, count), 0, 2 ** 20) * count
    scores = scores + jnp.arange(count, dtype=jnp.int32)
    order = jnp.argsort(scores, axis=-1, stable=True).astype(jnp.int32)
    return order[..., :TPG]


def draw_tile_count(key, part):
    key_level, key_raw, key_spot = jax.random.split(key, 3)
    lowest = (TPG + 1) // 2
    level = jax.random.randint(key_level, (N_DOM, N_BLK, 1), lowest, TPG + 1)
    raw = jax.random.randint(key_raw, (N_DOM, N_BLK, N_BLK), 0, 2 ** 20)
    counts = raw % level + 1
    spot = jax.random.randint(key_spot, (), 0, N_DOM * N_BLK * N_BLK)
    flat = jnp.arange(N_DOM * N_BLK * N_BLK, dtype=jnp.int32).reshape(N_DOM, N_BLK, N_BLK)
    return jnp.where(flat == spot, TPG, counts).astype(jnp.int32)


def draw_send_count(key, part):
    key_raw, key_src, key_grp, key_gap = jax.random.split(key, 4)
    counts = jax.random.randint(key_raw, (N_DOM, N_BLK, N_DOM), 0, SLOTS + 1)
    source = jax.random.randint(key_src, (), 0, N_DOM)
    group = jax.random.randint(key_grp, (), 0, N_BLK)
    target = (source + jax.random.randint(key_gap, (), 1, N_DOM)) % N_DOM
    src_ids = jnp.arange(N_DOM, dtype=jnp.int32)[:, None, None]
    grp_ids = jnp.arange(N_BLK, dtype=jnp.int32)[None, :, None]
    dst_ids = jnp.arange(N_DOM, dtype=jnp.int32)[None, None, :]
    chosen = (src_ids == source) & (grp_ids == group) & (dst_ids == target)
    counts = jnp.where(chosen, SLOTS, counts)
    counts = jnp.where(src_ids == dst_ids, 0, counts)
    return counts.astype(jnp.int32)


def with_ends(array, rng, least, top_value):
    index_at = [jax.random.randint(jax.random.fold_in(rng, axis), (), 0, length) for axis, length in enumerate(array.shape)]
    longest = array.shape.index(max(array.shape))
    beside = index_at[:longest] + [(index_at[longest] + 1) % array.shape[longest]] + index_at[longest + 1:]
    return array.at[tuple(index_at)].set(least).at[tuple(beside)].set(top_value)


def block_scale(own_key, extent, cuts, least, high):
    loudness = 1.0
    for axis_at, parts in cuts:
        heights = jax.random.uniform(jax.random.fold_in(jax.random.fold_in(own_key, 6), axis_at), (parts,), jnp.float32, least / len(cuts), high / len(cuts))
        loudness = loudness * jnp.repeat(jnp.exp(heights), extent[axis_at] // parts).reshape((-1,) + (1,) * (len(extent) - 1 - axis_at))
    return loudness


def scatter_about(own_key, shape, scale, bound, cuts=(), held_as=jnp.bfloat16):
    entries = scale * jax.random.normal(own_key, shape, jnp.float32)
    if cuts:
        entries = entries * block_scale(own_key, shape, cuts, -0.22, 0.18)
    return jnp.clip(entries, -bound, bound).astype(held_as)


def setup_inputs(seed: int = 0) -> dict:
    streams_of = jax.random.split(jax.random.key(seed), 11)
    features = scatter_about(streams_of[0], (N_DOM, VERTS, F), 1.0, 6.0, ((0, 8), (1, 4)))
    weight = scatter_about(streams_of[1], (F, F), F ** -0.5, 0.375)
    tiles = scatter_about(streams_of[2], (N_DOM, N_BLK, N_BLK, TPG, TILE, TILE), ((2.0 * ROWS / (TILE * TILE * N_BLK * TPG)) ** 0.5), 0.3046875, ((0, 8), (1, 4)))
    tile_pos = draw_tile_pos(jax.random.fold_in(streams_of[10], 71), 0)
    tile_count = draw_tile_count(jax.random.fold_in(streams_of[10], 71), 0)
    send_list = with_ends(jax.random.randint(streams_of[5], (N_DOM, N_BLK, N_DOM, SLOTS), 0, ROWS), jax.random.fold_in(streams_of[5], 1), 0, ROWS - 1).astype(jnp.int32)
    send_count = draw_send_count(jax.random.fold_in(streams_of[10], 71), 0)
    owner_map = with_ends(jax.random.randint(streams_of[7], (N_DOM, N_BLK, N_DOM, SLOTS), 0, ROWS), jax.random.fold_in(streams_of[7], 1), 0, ROWS - 1).astype(jnp.int32)
    halo_weight = jnp.clip(jnp.exp(math.log(1.0) - 1.3862944 * jax.random.uniform(streams_of[8], (N_DOM, N_BLK, N_DOM, SLOTS), jnp.float32) ** block_scale(streams_of[8], (N_DOM, N_BLK, N_DOM, SLOTS), ((0, 8), (1, 4)), -0.2, 0.2)), 0.25, 1.0)
    cotangent = scatter_about(streams_of[9], (N_DOM, VERTS, F), 1.0, 6.0, ((0, 8), (1, 4)))
    return {"features": features, "weight": weight, "tiles": tiles, "tile_pos": tile_pos, "tile_count": tile_count, "send_list": send_list, "send_count": send_count, "owner_map": owner_map, "halo_weight": halo_weight, "cotangent": cotangent}


def spread_rows(tile_set, positions, counts, panel, per):
    groups, slots = positions.shape
    tile = tile_set.shape[-1]
    width = panel.shape[-1]
    grid = panel.reshape(groups, per, tile, width)
    column = positions % per
    row_tile = positions // per
    picked = grid[jnp.arange(groups)[:, None], column]
    product = jnp.einsum("gtij,gtjf->gtif", tile_set.astype(jnp.float32), picked.astype(jnp.float32))
    live = jnp.arange(slots)[None, :] < counts[:, None]
    select = ((row_tile[..., None] == jnp.arange(per)[None, None, :]) & live[..., None]).astype(jnp.float32)
    return jnp.einsum("gtif,gtr->rif", product, select).reshape(per * tile, width)


def spread_cols(tile_set, positions, counts, grad_rows, per):
    groups, slots = positions.shape
    tile = tile_set.shape[-1]
    width = grad_rows.shape[-1]
    grid = grad_rows.reshape(per, tile, width)
    column = positions % per
    row_tile = positions // per
    picked = grid[row_tile]
    product = jnp.einsum("gtij,gtif->gtjf", tile_set.astype(jnp.float32), picked.astype(jnp.float32))
    live = jnp.arange(slots)[None, :] < counts[:, None]
    select = ((column[..., None] == jnp.arange(per)[None, None, :]) & live[..., None]).astype(jnp.float32)
    return jnp.einsum("gtjf,gtc->gcjf", product, select).reshape(groups * per * tile, width)


def reference(features, weight, tiles, tile_pos, tile_count, send_list, send_count, owner_map, halo_weight, cotangent):
    n_dom, verts, width = features.shape
    n_blk = tiles.shape[1]
    rows = verts // n_blk
    tile = tiles.shape[-1]
    per = rows // tile
    slots = send_list.shape[-1]
    projected = jnp.dot(features.reshape(-1, width), weight, preferred_element_type=jnp.float32)
    projected = projected.astype(jnp.bfloat16).reshape(n_dom, verts, width)

    def forward_one(index):
        part_id = index // n_blk
        group = index % n_blk
        return spread_rows(tiles[part_id, group], tile_pos[part_id, group], tile_count[part_id, group], projected[part_id], per)

    local = lax.map(forward_one, jnp.arange(n_dom * n_blk)).reshape(n_dom, n_blk, rows, width)

    proj_blocks = projected.reshape(n_dom, n_blk, rows, width)
    src_index = jnp.arange(n_dom)[:, None, None, None]
    grp_index = jnp.arange(n_blk)[None, :, None, None]
    live = (jnp.arange(slots)[None, None, None, :] < send_count[..., None])[..., None]
    sent = jnp.where(live, proj_blocks[src_index, grp_index, send_list], jnp.zeros((), jnp.bfloat16))
    received = jnp.transpose(sent, (2, 1, 0, 3, 4))

    def halo_one(target):
        incoming = received[target].astype(jnp.float32) * halo_weight[target][..., None]
        flat_owner = (jnp.arange(n_blk)[:, None, None] * rows + owner_map[target]).reshape(-1)
        summed = jax.ops.segment_sum(incoming.reshape(-1, width), flat_owner, num_segments=n_blk * rows)
        return summed.reshape(n_blk, rows, width)

    halo_sum = lax.map(halo_one, jnp.arange(n_dom))
    aggregated = local + halo_sum
    layer_out = aggregated.astype(jnp.bfloat16).reshape(n_dom, verts, width)

    grad_blocks = cotangent.reshape(n_dom, n_blk, rows, width)
    back = halo_weight[..., None] * grad_blocks[src_index, grp_index, owner_map].astype(jnp.float32)
    back = back.astype(jnp.bfloat16)
    returned = jnp.transpose(back, (2, 1, 0, 3, 4))
    returned = jnp.where(live, returned, jnp.zeros((), jnp.bfloat16))

    def back_one(source):
        flat_rows = (jnp.arange(n_blk)[:, None, None] * rows + send_list[source]).reshape(-1)
        summed = jax.ops.segment_sum(returned[source].astype(jnp.float32).reshape(-1, width), flat_rows, num_segments=n_blk * rows)
        return summed

    halo_back = lax.map(back_one, jnp.arange(n_dom))

    def grad_part(part_id):
        def step(carry, group):
            grad_rows = lax.dynamic_slice_in_dim(cotangent[part_id], group * rows, rows, 0)
            partial_value = spread_cols(tiles[part_id, group], tile_pos[part_id, group], tile_count[part_id, group], grad_rows, per)
            rounded = lax.optimization_barrier(partial_value.astype(jnp.bfloat16))
            return carry + rounded.astype(jnp.float32), None

        start = jnp.zeros((verts, width), jnp.float32)
        total, unused = lax.scan(step, start, jnp.arange(n_blk))
        return total

    local_grad = lax.map(grad_part, jnp.arange(n_dom))
    proj_grad = (local_grad + halo_back).astype(jnp.bfloat16)
    flat_grad = proj_grad.reshape(-1, width)
    feature_grad = jnp.dot(flat_grad, weight.T, preferred_element_type=jnp.float32).astype(jnp.bfloat16)
    feature_grad = feature_grad.reshape(n_dom, verts, width)
    weight_grad = jnp.dot(features.reshape(-1, width).T, flat_grad, preferred_element_type=jnp.float32)
    weight_grad = weight_grad * (float(n_dom * verts) ** -0.5)
    return layer_out, feature_grad, weight_grad
```

```python
import functools
import jax
import jax.numpy as jnp
from jax import lax
from jax.experimental import pallas as pl
from jax.experimental.pallas import tpu as pltpu
from jax.sharding import PartitionSpec as P

BF16 = jnp.bfloat16
F32 = jnp.float32
VMEM = pl.BlockSpec(memory_space=pltpu.VMEM)
SMEM = pl.BlockSpec(memory_space=pltpu.SMEM)
MIB = 1 << 20


def swap(value, axis, bit):
    return lax.ppermute(value, axis, [(i, i ^ bit) for i in range(lax.axis_size(axis))])


def bits_of(size):
    return [1 << k for k in range(size.bit_length() - 1)]


def matmul(left, right, left_dim, right_dim):
    return lax.dot_general(
        left, right, (((left_dim,), (right_dim,)), ((), ())), preferred_element_type=F32
    )


def one_hot(rows, index):
    return lax.broadcasted_iota(jnp.int32, (rows, index.shape[1]), 0) == index


def halo_kernel(feats, grad, send_index, owner, edge, out):
    rows, width = feats.shape
    peers, both, unused = out.shape
    slots = both // 2
    sent = matmul(one_hot(rows, send_index[...]).astype(BF16), feats[...], 0, 0)
    out[:, :slots, :] = sent.astype(BF16).reshape(peers, slots, width)
    weights = jnp.where(one_hot(rows, owner[...]), edge[...], 0.0).astype(BF16)
    back = matmul(weights, grad[...], 0, 0)
    out[:, slots:, :] = back.astype(BF16).reshape(peers, slots, width)


def adjacency_kernel(blk, pos, count, tiles, grad, dense, keep, send):
    groups, slots, tile, unused = tiles.shape
    rows, width = grad.shape
    per = rows // tile
    dense[...] = jnp.zeros_like(dense)
    for j in range(groups):
        c = blk[0] ^ j
        for t in range(slots):
            spot = pos[c * slots + t]
            row = pl.multiple_of((spot // per) * tile, tile)
            column = pl.multiple_of(j * rows + (spot % per) * tile, tile)
            live = t < count[c]
            dense[pl.ds(row, tile), pl.ds(column, tile)] = jnp.where(
                live, tiles[c, t], jnp.zeros((), BF16)
            )
    turned = grad[...].T
    for j in range(groups):
        part = matmul(turned, dense[:, j * rows : (j + 1) * rows], 1, 0).astype(BF16)
        (send if j % 2 else keep)[j // 2] = part


def forward_kernel(groups, blk, dense, halo, owner, edge, grad, *refs):
    panels, (agg, keep, send, term) = refs[:groups], refs[groups:]
    rows, width = grad.shape
    slots = halo.shape[1] // 2
    total = matmul(dense[:, :rows], panels[0][...], 1, 0)
    for j in range(1, groups):
        total += matmul(dense[:, j * rows : (j + 1) * rows], panels[j][...], 1, 0)
    weights = jnp.where(one_hot(rows, owner[...]), edge[...], 0.0).astype(BF16)
    total += matmul(weights, halo[:, :slots, :].reshape(-1, width), 1, 0)
    rounded = total.astype(BF16)
    agg[...] = rounded
    term[...] = matmul(rounded, grad[...], 0, 0)
    half = width // 2
    core = blk[0] % 2
    keep[...] = term[pl.ds(pl.multiple_of(core * half, half), half), :].astype(BF16)
    send[...] = term[pl.ds(pl.multiple_of((1 - core) * half, half), half), :].astype(BF16)


def output_kernel(agg, weight, out):
    out[...] = matmul(agg[...], weight[...], 1, 0).astype(BF16)


def backward_kernel(first, second, third, halo, send_index, weight, out):
    rows, width = out.shape
    slots = halo.shape[1] // 2
    local = first[...].astype(F32) + second[...].astype(F32) + third[...].astype(F32)
    total = local.T + matmul(
        one_hot(rows, send_index[...]).astype(BF16), halo[:, slots:, :].reshape(-1, width), 1, 0
    )
    out[...] = matmul(total.astype(BF16), weight[...], 1, 1).astype(BF16)


def call(kernel, outs, specs, limit, scratch=()):
    return pl.pallas_call(
        kernel,
        out_shape=[jax.ShapeDtypeStruct(shape, dtype) for shape, dtype in outs],
        in_specs=specs,
        out_specs=[VMEM] * len(outs),
        scratch_shapes=list(scratch),
        compiler_params=pltpu.CompilerParams(vmem_limit_bytes=limit),
    )


def add(left, right):
    return (left.astype(F32) + right.astype(F32)).astype(BF16)


def on_device(
    features,
    weight,
    tiles,
    tile_pos,
    tile_count,
    send_list,
    send_count,
    owner_map,
    halo_weight,
    cotangent,
):
    groups, peers = lax.axis_size("blk"), lax.axis_size("dom")
    feats, grad = features[0], cotangent[0]
    rows, width = feats.shape
    slots = send_list.shape[-1]
    links = peers * slots
    me = lax.axis_index("blk").astype(jnp.int32)
    blk = me.reshape(1)
    live = jnp.arange(slots)[None, :] < send_count[0, 0][:, None]
    send_index = jnp.where(live, send_list[0, 0], -1).reshape(1, links)
    owner = owner_map[0, 0].reshape(1, links)
    edge = halo_weight[0, 0].reshape(1, links)

    (outgoing,) = call(
        halo_kernel, [((peers, 2 * slots, width), BF16)], [VMEM] * 5, 16 * MIB
    )(feats, grad, send_index, owner, edge)
    halo = lax.all_to_all(outgoing, "dom", split_axis=0, concat_axis=0, tiled=True)

    panels = {0: feats}
    for bit in reversed(bits_of(groups)):
        for j in list(panels):
            panels[j ^ bit] = swap(panels[j], "blk", bit)

    half = groups // 2
    dense, keep, send = call(
        adjacency_kernel,
        [
            ((rows, groups * rows), BF16),
            ((half, width, rows), BF16),
            ((half, width, rows), BF16),
        ],
        [SMEM] * 3 + [VMEM] * 2,
        (8 + 4 * groups) * MIB,
    )(blk, tile_pos.reshape(-1), tile_count.reshape(-1), tiles[0, 0], grad)
    got = swap(send, "blk", 1)
    for bit in bits_of(groups)[1:]:
        later = [add(keep[j], got[j]) for j in range(1, keep.shape[0], 2)]
        first = [(keep[j], got[j]) for j in range(0, keep.shape[0], 2)]
        if len(first) == 1:
            third = swap(later[0], "blk", bit)
            first, second = first[0]
        else:
            keep = jnp.stack([add(*pair) for pair in first])
            got = swap(jnp.stack(later), "blk", bit)

    agg, kept, sent = call(
        functools.partial(forward_kernel, groups),
        [((rows, width), BF16), ((width // 2, width), BF16), ((width // 2, width), BF16)],
        [SMEM] + [VMEM] * (5 + groups),
        (8 + 4 * groups) * MIB,
        [pltpu.VMEM((width, width), F32)],
    )(blk, dense, halo, owner, edge, grad, *[panels[j] for j in range(groups)])
    term = add(kept, swap(sent, "blk", 1))
    for bit in bits_of(peers):
        term = add(term, swap(term, "dom", bit))
    for bit in bits_of(groups)[1:]:
        term = add(term, swap(term, "blk", bit))
    other = swap(term, "blk", 1)
    scale = float(groups * peers * rows) ** (-0.5)
    low = jnp.where(me % 2 == 0, term, other)
    high = jnp.where(me % 2 == 0, other, term)
    weight_grad = jnp.concatenate([low, high]).astype(F32) * scale

    (layer_out,) = call(output_kernel, [((rows, width), BF16)], [VMEM] * 2, 16 * MIB)(agg, weight)
    (feature_grad,) = call(backward_kernel, [((rows, width), BF16)], [VMEM] * 6, 16 * MIB)(
        first, second, third, halo, send_index, weight
    )
    return layer_out[None], feature_grad[None], weight_grad


def solution(mesh):
    return jax.shard_map(
        on_device,
        mesh=mesh,
        in_specs=(
            P("dom", "blk", None),
            P(),
            P("dom", "blk", None, None, None, None),
            P("dom", "blk", None, None),
            P("dom", "blk", None),
            P("dom", "blk", None, None),
            P("dom", "blk", None),
            P("dom", "blk", None, None),
            P("dom", "blk", None, None),
            P("dom", "blk", None),
        ),
        out_specs=(P("dom", "blk", None), P("dom", "blk", None), P()),
        check_vma=False,
    )
```

```python
import functools
import jax
import jax.numpy as jnp
from jax import lax
from jax.experimental import pallas as pl
from jax.experimental.pallas import tpu as pltpu
from jax.sharding import PartitionSpec as P

BF16 = jnp.bfloat16
F32 = jnp.float32
VMEM = pl.BlockSpec(memory_space=pltpu.VMEM)
SMEM = pl.BlockSpec(memory_space=pltpu.SMEM)
HBM = pl.BlockSpec(memory_space=pltpu.HBM)
MIB = 1 << 20


def swap(value, axis, bit):
    return lax.ppermute(value, axis, [(i, i ^ bit) for i in range(lax.axis_size(axis))])


def swap_bits(value, bits):
    groups, peers = lax.axis_size("blk"), lax.axis_size("dom")
    b_bits = sum(bit for axis, bit in bits if axis == "blk")
    d_bits = sum(bit for axis, bit in bits if axis == "dom")
    pairs = [
        (b * peers + d, (b ^ b_bits) * peers + (d ^ d_bits))
        for b in range(groups)
        for d in range(peers)
    ]
    return lax.ppermute(value, ("blk", "dom"), pairs)


def bits_of(size):
    return [1 << k for k in range(size.bit_length() - 1)]


def matmul(left, right, left_dim, right_dim):
    return lax.dot_general(
        left, right, (((left_dim,), (right_dim,)), ((), ())), preferred_element_type=F32
    )


def one_hot(rows, index):
    return lax.broadcasted_iota(jnp.int32, (rows, index.shape[1]), 0) == index


def flat(rows):
    return jnp.concatenate([rows[q : q + 1, :] for q in range(rows.shape[0])], axis=1)


def send_index_of(send_list, send_count):
    peers, slots = send_list.shape
    peer = lax.broadcasted_iota(jnp.int32, (peers, slots), 0)
    slot = lax.broadcasted_iota(jnp.int32, (peers, slots), 1)
    count = jnp.zeros((peers, slots), jnp.int32)
    for q in range(peers):
        count = jnp.where(peer == q, send_count[q], count)
    return flat(jnp.where(slot < count, send_list[...], -1))


def fetch(pairs, sems):
    copies = [pltpu.make_async_copy(src, dst, sems.at[i]) for i, (src, dst) in enumerate(pairs)]
    for copy in copies:
        copy.start()
    return copies


def halo_kernel(feats_in, grad_in, send_in, count_in, owner_in, edge_in, out, *scratch):
    feats, grad, send, count, owner, edge, sems = scratch
    sources = (feats_in, grad_in, send_in, count_in, owner_in, edge_in)
    for copy in fetch(list(zip(sources, scratch)), sems):
        copy.wait()
    rows, width = feats.shape
    peers, both, unused = out.shape
    slots = both // 2
    pick = one_hot(rows, send_index_of(send, count)).astype(BF16)
    sent = matmul(pick, feats[...], 0, 0)
    out[:, :slots, :] = sent.astype(BF16).reshape(peers, slots, width)
    weights = jnp.where(one_hot(rows, flat(owner)), flat(edge), 0.0).astype(BF16)
    back = matmul(weights, grad[...], 0, 0)
    out[:, slots:, :] = back.astype(BF16).reshape(peers, slots, width)


def build(blk, dense, pos, count, tiles, rows):
    groups, slots, tile, unused = tiles.shape
    per = rows // tile
    for j in range(groups):
        c = blk[0] ^ j
        for t in range(slots):
            spot = pos[c, t]
            row = pl.multiple_of((spot // per) * tile, tile)
            column = pl.multiple_of(j * rows + (spot % per) * tile, tile)
            live = t < count[c]
            dense[pl.ds(row, tile), pl.ds(column, tile)] = jnp.where(
                live, tiles[c, t], jnp.zeros((), BF16)
            )


def backward_terms_kernel(groups, blk, pos_in, count_in, tiles_in, grad_in, *refs):
    (send, *keep), (dense, sems, *homes) = refs[: 1 + groups // 2], refs[1 + groups // 2 :]
    pos, count, tiles, grad = homes
    copies = fetch(list(zip((pos_in, count_in, tiles_in, grad_in), homes)), sems)
    rows, width = grad.shape
    dense[...] = jnp.zeros_like(dense)
    for copy in copies:
        copy.wait()
    build(blk, dense, pos, count, tiles, rows)
    turned = grad[...].T
    for j in range(groups):
        part = matmul(turned, dense[:, j * rows : (j + 1) * rows], 1, 0).astype(BF16)
        if j % 2:
            send[j // 2] = part
        else:
            keep[j // 2][...] = part


def local_kernel(groups, blk, pos_in, count_in, tiles_in, *refs):
    panels_in, (local, dense, sems, *homes) = refs[:groups], refs[groups:]
    pos, count, tiles, *panels = homes
    copies = fetch(list(zip((pos_in, count_in, tiles_in, *panels_in), homes)), sems)
    rows, width = local.shape
    dense[...] = jnp.zeros_like(dense)
    for copy in copies:
        copy.wait()
    build(blk, dense, pos, count, tiles, rows)
    value = matmul(dense[:, :rows], panels[0][...], 1, 0)
    for j in range(1, groups):
        value += matmul(dense[:, j * rows : (j + 1) * rows], panels[j][...], 1, 0)
    local[...] = value


def forward_kernel(blk, local, halo, owner, edge, grad, agg, keep, send, term):
    rows, width = grad.shape
    slots = halo.shape[1] // 2
    weights = jnp.where(one_hot(rows, flat(owner)), flat(edge), 0.0).astype(BF16)
    total = local[...] + matmul(weights, halo[:, :slots, :].reshape(-1, width), 1, 0)
    rounded = total.astype(BF16)
    agg[...] = rounded
    term[...] = matmul(rounded, grad[...], 0, 0)
    half = width // 2
    core = blk[0] % 2
    keep[...] = term[pl.ds(pl.multiple_of(core * half, half), half), :].astype(BF16)
    send[...] = term[pl.ds(pl.multiple_of((1 - core) * half, half), half), :].astype(BF16)


def output_kernel(agg, weight, out):
    out[...] = matmul(agg[...], weight[...], 1, 0).astype(BF16)


def backward_kernel(send_count, first, others, third, halo, send_list, weight, out):
    rows, width = out.shape
    slots = halo.shape[1] // 2
    local = first[...].astype(F32) + others[0].astype(F32) + third[...].astype(F32)
    total = local.T + matmul(
        one_hot(rows, send_index_of(send_list, send_count)).astype(BF16),
        halo[:, slots:, :].reshape(-1, width),
        1,
        0,
    )
    out[...] = matmul(total.astype(BF16), weight[...], 1, 1).astype(BF16)


def call(kernel, outs, specs, limit, scratch=()):
    return pl.pallas_call(
        kernel,
        out_shape=[jax.ShapeDtypeStruct(shape, dtype) for shape, dtype in outs],
        in_specs=specs,
        out_specs=[VMEM] * len(outs),
        scratch_shapes=list(scratch),
        compiler_params=pltpu.CompilerParams(vmem_limit_bytes=limit),
    )


def add(left, right):
    return (left.astype(F32) + right.astype(F32)).astype(BF16)


def on_device(
    features,
    weight,
    tiles,
    tile_pos,
    tile_count,
    send_list,
    send_count,
    owner_map,
    halo_weight,
    cotangent,
):
    groups, peers = lax.axis_size("blk"), lax.axis_size("dom")
    feats, grad = features[0], cotangent[0]
    rows, width = feats.shape
    slots = send_list.shape[-1]
    links = peers * slots
    me = lax.axis_index("blk").astype(jnp.int32)
    blk = me.reshape(1)
    sends, send_live = send_list[0, 0], send_count[0, 0]
    owner, edge = owner_map[0, 0], halo_weight[0, 0]

    feats_far = swap(feats, "blk", groups // 2)
    (outgoing,) = call(
        halo_kernel,
        [((peers, 2 * slots, width), BF16)],
        [HBM] * 6,
        64 * MIB,
        [
            pltpu.VMEM((rows, width), BF16),
            pltpu.VMEM((rows, width), BF16),
            pltpu.VMEM((peers, slots), jnp.int32),
            pltpu.SMEM((peers,), jnp.int32),
            pltpu.VMEM((peers, slots), jnp.int32),
            pltpu.VMEM((peers, slots), F32),
            pltpu.SemaphoreType.DMA((6,)),
        ],
    )(feats, grad, sends, send_live, owner, edge)
    outgoing, near, tile_set = lax.optimization_barrier((outgoing, feats, tiles[0, 0]))
    halo = lax.all_to_all(outgoing, "dom", split_axis=0, concat_axis=0, tiled=True)

    panels = {0: near, groups // 2: feats_far}
    for bit in reversed(bits_of(groups // 2)):
        for j in list(panels):
            panels[j ^ bit] = swap(panels[j], "blk", bit)

    half = groups // 2
    tile_scratch = [
        pltpu.SMEM(tile_pos.shape[2:], jnp.int32),
        pltpu.SMEM(tile_count.shape[2:], jnp.int32),
        pltpu.VMEM(tiles.shape[2:], BF16),
    ]
    dense = pltpu.VMEM((rows, groups * rows), BF16)
    panel = pltpu.VMEM((rows, width), BF16)
    send, *keep = call(
        functools.partial(backward_terms_kernel, groups),
        [((half, width, rows), BF16)] + [((width, rows), BF16)] * half,
        [SMEM] + [HBM] * 4,
        64 * MIB,
        [dense, pltpu.SemaphoreType.DMA((4,)), *tile_scratch, panel],
    )(blk, tile_pos[0, 0], tile_count[0, 0], tile_set, grad)
    send, tile_set = lax.optimization_barrier((send, tile_set))
    got = swap(send, "blk", 1)
    (local,) = call(
        functools.partial(local_kernel, groups),
        [((rows, width), F32)],
        [SMEM] + [HBM] * (3 + groups),
        61 * MIB,
        [dense, pltpu.SemaphoreType.DMA((3 + groups,)), *tile_scratch] + [panel] * groups,
    )(
        blk,
        tile_pos[0, 0],
        tile_count[0, 0],
        tile_set,
        *[panels[j] for j in range(groups)],
    )

    agg, kept, sent = call(
        forward_kernel,
        [((rows, width), BF16), ((width // 2, width), BF16), ((width // 2, width), BF16)],
        [SMEM] + [VMEM] * 5,
        16 * MIB,
        [pltpu.VMEM((width, width), F32)],
    )(blk, local, halo, owner, edge, grad)
    other = swap(sent, "blk", 1)
    inner = bits_of(groups)[1:]
    for bit in inner:
        later = [add(keep[j], got[j]) for j in range(1, len(keep), 2)]
        if len(keep) == 2:
            third = swap(later[0], "blk", bit)
        else:
            keep = [add(keep[j], got[j]) for j in range(0, len(keep), 2)]
            got = swap(jnp.stack(later), "blk", bit)
    term = add(kept, other)
    bits = [("dom", bit) for bit in reversed(bits_of(peers))] + [("blk", bit) for bit in inner]
    fours = [bits[i : i + 2] for i in range(0, len(bits), 2)]
    for i, four in enumerate(fours):
        first, last = i == 0, i == len(fours) - 1
        if first:
            term, agg = lax.optimization_barrier((term, agg))
            (layer_out,) = call(output_kernel, [((rows, width), BF16)], [VMEM] * 2, 16 * MIB)(
                agg, weight
            )
        if last:
            (feature_grad,) = call(
                backward_kernel, [((rows, width), BF16)], [SMEM] + [VMEM] * 6, 16 * MIB
            )(send_live, keep[0], got, third, halo, sends, weight)
        others = [swap_bits(term, four[:1])]
        if len(four) == 2:
            others += [swap_bits(term, four[1:]), swap_bits(term, four)]
        if first:
            others, layer_out = lax.optimization_barrier((others, layer_out))
        if last:
            others, feature_grad = lax.optimization_barrier((others, feature_grad))
        wide = [value.astype(F32) for value in (term, *others)]
        total = wide[0] + wide[1]
        if len(four) == 2:
            total += wide[2] + wide[3]
        term = total.astype(BF16)
    other = swap(term, "blk", 1)
    scale = float(groups * peers * rows) ** (-0.5)
    low = jnp.where(me % 2 == 0, term, other)
    high = jnp.where(me % 2 == 0, other, term)
    weight_grad = jnp.concatenate([low, high]).astype(F32) * scale
    return layer_out[None], feature_grad[None], weight_grad


def solution(mesh):
    return jax.shard_map(
        on_device,
        mesh=mesh,
        in_specs=(
            P("dom", "blk", None),
            P(),
            P("dom", "blk", None, None, None, None),
            P("dom", "blk", None, None),
            P("dom", "blk", None),
            P("dom", "blk", None, None),
            P("dom", "blk", None),
            P("dom", "blk", None, None),
            P("dom", "blk", None, None),
            P("dom", "blk", None),
        ),
        out_specs=(P("dom", "blk", None), P("dom", "blk", None), P()),
        check_vma=False,
    )
```

```python
import functools
import jax
import jax.numpy as jnp
from jax import lax
from jax.experimental import pallas as pl
from jax.experimental.pallas import tpu as pltpu
from jax.sharding import PartitionSpec as P

BF16 = jnp.bfloat16
F32 = jnp.float32
VMEM = pl.BlockSpec(memory_space=pltpu.VMEM)
SMEM = pl.BlockSpec(memory_space=pltpu.SMEM)
HBM = pl.BlockSpec(memory_space=pltpu.HBM)
MIB = 1 << 20


def swap(value, axis, bit):
    return lax.ppermute(value, axis, [(i, i ^ bit) for i in range(lax.axis_size(axis))])


def swap_bits(value, bits):
    groups, peers = lax.axis_size("blk"), lax.axis_size("dom")
    b_bits = sum(bit for axis, bit in bits if axis == "blk")
    d_bits = sum(bit for axis, bit in bits if axis == "dom")
    pairs = [
        (b * peers + d, (b ^ b_bits) * peers + (d ^ d_bits))
        for b in range(groups)
        for d in range(peers)
    ]
    return lax.ppermute(value, ("blk", "dom"), pairs)


def bits_of(size):
    return [1 << k for k in range(size.bit_length() - 1)]


def matmul(left, right, left_dim, right_dim):
    return lax.dot_general(
        left, right, (((left_dim,), (right_dim,)), ((), ())), preferred_element_type=F32
    )


def one_hot(rows, index):
    return lax.broadcasted_iota(jnp.int32, (rows, index.shape[1]), 0) == index


def flat(rows):
    return jnp.concatenate([rows[q : q + 1, :] for q in range(rows.shape[0])], axis=1)


def send_index_of(send_list, send_count):
    peers, slots = send_list.shape
    peer = lax.broadcasted_iota(jnp.int32, (peers, slots), 0)
    slot = lax.broadcasted_iota(jnp.int32, (peers, slots), 1)
    count = jnp.zeros((peers, slots), jnp.int32)
    for q in range(peers):
        count = jnp.where(peer == q, send_count[q], count)
    return flat(jnp.where(slot < count, send_list[...], -1))


def fetch(pairs, sems):
    copies = [pltpu.make_async_copy(src, dst, sems.at[i]) for i, (src, dst) in enumerate(pairs)]
    for copy in copies:
        copy.start()
    return copies


def halo_kernel(feats_in, grad_in, send_in, count_in, owner_in, edge_in, out, *scratch):
    feats, grad, send, count, owner, edge, sems = scratch
    sources = (feats_in, grad_in, send_in, count_in, owner_in, edge_in)
    for copy in fetch(list(zip(sources, scratch)), sems):
        copy.wait()
    rows, width = feats.shape
    peers, both, unused = out.shape
    slots = both // 2
    pick = one_hot(rows, send_index_of(send, count)).astype(BF16)
    sent = matmul(pick, feats[...], 0, 0)
    out[:, :slots, :] = sent.astype(BF16).reshape(peers, slots, width)
    weights = jnp.where(one_hot(rows, flat(owner)), flat(edge), 0.0).astype(BF16)
    back = matmul(weights, grad[...], 0, 0)
    out[:, slots:, :] = back.astype(BF16).reshape(peers, slots, width)


def adjacency_kernel(groups, blk, pos_in, count_in, tiles_in, grad_in, *refs):
    panels_in, refs = refs[:groups], refs[groups:]
    (local, send, *keep), refs = refs[: 2 + groups // 2], refs[2 + groups // 2 :]
    dense, sems, *homes = refs
    pos, count, tiles, grad, *panels = homes
    copies = fetch(list(zip((pos_in, count_in, tiles_in, grad_in, *panels_in), homes)), sems)
    unused, slots, tile, unused = tiles.shape
    rows, width = grad.shape
    per = rows // tile
    dense[...] = jnp.zeros_like(dense)
    for copy in copies:
        copy.wait()
    for j in range(groups):
        c = blk[0] ^ j
        for t in range(slots):
            spot = pos[c, t]
            row = pl.multiple_of((spot // per) * tile, tile)
            column = pl.multiple_of(j * rows + (spot % per) * tile, tile)
            live = t < count[c]
            dense[pl.ds(row, tile), pl.ds(column, tile)] = jnp.where(
                live, tiles[c, t], jnp.zeros((), BF16)
            )
    turned = grad[...].T
    for j in range(groups):
        part = matmul(turned, dense[:, j * rows : (j + 1) * rows], 1, 0).astype(BF16)
        if j % 2:
            send[j // 2] = part
        else:
            keep[j // 2][...] = part
    value = matmul(dense[:, :rows], panels[0][...], 1, 0)
    for j in range(1, groups):
        value += matmul(dense[:, j * rows : (j + 1) * rows], panels[j][...], 1, 0)
    local[...] = value


def forward_kernel(blk, local, halo, owner, edge, grad, agg, keep, send, term):
    rows, width = grad.shape
    slots = halo.shape[1] // 2
    weights = jnp.where(one_hot(rows, flat(owner)), flat(edge), 0.0).astype(BF16)
    total = local[...] + matmul(weights, halo[:, :slots, :].reshape(-1, width), 1, 0)
    rounded = total.astype(BF16)
    agg[...] = rounded
    term[...] = matmul(rounded, grad[...], 0, 0)
    half = width // 2
    core = blk[0] % 2
    keep[...] = term[pl.ds(pl.multiple_of(core * half, half), half), :].astype(BF16)
    send[...] = term[pl.ds(pl.multiple_of((1 - core) * half, half), half), :].astype(BF16)


def output_kernel(agg, weight, out):
    out[...] = matmul(agg[...], weight[...], 1, 0).astype(BF16)


def backward_kernel(send_count, first, others, third, halo, send_list, weight, out):
    rows, width = out.shape
    slots = halo.shape[1] // 2
    local = first[...].astype(F32) + others[0].astype(F32) + third[...].astype(F32)
    total = local.T + matmul(
        one_hot(rows, send_index_of(send_list, send_count)).astype(BF16),
        halo[:, slots:, :].reshape(-1, width),
        1,
        0,
    )
    out[...] = matmul(total.astype(BF16), weight[...], 1, 1).astype(BF16)


def call(kernel, outs, specs, limit, scratch=(), flops=1):
    return pl.pallas_call(
        kernel,
        out_shape=[jax.ShapeDtypeStruct(shape, dtype) for shape, dtype in outs],
        in_specs=specs,
        out_specs=[VMEM] * len(outs),
        scratch_shapes=list(scratch),
        cost_estimate=pl.CostEstimate(flops=flops, bytes_accessed=1, transcendentals=0),
        compiler_params=pltpu.CompilerParams(vmem_limit_bytes=limit),
    )


def add(left, right):
    return (left.astype(F32) + right.astype(F32)).astype(BF16)


def on_device(
    features,
    weight,
    tiles,
    tile_pos,
    tile_count,
    send_list,
    send_count,
    owner_map,
    halo_weight,
    cotangent,
):
    groups, peers = lax.axis_size("blk"), lax.axis_size("dom")
    feats, grad = features[0], cotangent[0]
    rows, width = feats.shape
    slots = send_list.shape[-1]
    links = peers * slots
    me = lax.axis_index("blk").astype(jnp.int32)
    blk = me.reshape(1)
    sends, send_live = send_list[0, 0], send_count[0, 0]
    owner, edge = owner_map[0, 0], halo_weight[0, 0]

    feats_far = swap(feats, "blk", groups // 2)
    (outgoing,) = call(
        halo_kernel,
        [((peers, 2 * slots, width), BF16)],
        [HBM] * 6,
        64 * MIB,
        [
            pltpu.VMEM((rows, width), BF16),
            pltpu.VMEM((rows, width), BF16),
            pltpu.VMEM((peers, slots), jnp.int32),
            pltpu.SMEM((peers,), jnp.int32),
            pltpu.VMEM((peers, slots), jnp.int32),
            pltpu.VMEM((peers, slots), F32),
            pltpu.SemaphoreType.DMA((6,)),
        ],
    )(feats, grad, sends, send_live, owner, edge)
    outgoing, near, tile_set = lax.optimization_barrier((outgoing, feats, tiles[0, 0]))
    halo = lax.all_to_all(outgoing, "dom", split_axis=0, concat_axis=0, tiled=True)

    panels = {0: near, groups // 2: feats_far}
    for bit in reversed(bits_of(groups // 2)):
        for j in list(panels):
            panels[j ^ bit] = swap(panels[j], "blk", bit)

    half = groups // 2
    panel = pltpu.VMEM((rows, width), BF16)
    local, send, *keep = call(
        functools.partial(adjacency_kernel, groups),
        [((rows, width), F32), ((half, width, rows), BF16)] + [((width, rows), BF16)] * half,
        [SMEM] + [HBM] * (4 + groups),
        61 * MIB,
        [
            pltpu.VMEM((rows, groups * rows), BF16),
            pltpu.SemaphoreType.DMA((4 + groups,)),
            pltpu.SMEM(tile_pos.shape[2:], jnp.int32),
            pltpu.SMEM(tile_count.shape[2:], jnp.int32),
            pltpu.VMEM(tiles.shape[2:], BF16),
        ]
        + [panel] * (1 + groups),
    )(
        blk,
        tile_pos[0, 0],
        tile_count[0, 0],
        tile_set,
        grad,
        *[panels[j] for j in range(groups)],
    )
    got = swap(send, "blk", 1)

    agg, kept, sent = call(
        forward_kernel,
        [((rows, width), BF16), ((width // 2, width), BF16), ((width // 2, width), BF16)],
        [SMEM] + [VMEM] * 5,
        16 * MIB,
        [pltpu.VMEM((width, width), F32)],
        flops=2 * 10**10,
    )(blk, local, halo, owner, edge, grad)
    other = swap(sent, "blk", 1)
    inner = bits_of(groups)[1:]
    for bit in inner:
        later = [add(keep[j], got[j]) for j in range(1, len(keep), 2)]
        if len(keep) == 2:
            third = swap(later[0], "blk", bit)
        else:
            keep = [add(keep[j], got[j]) for j in range(0, len(keep), 2)]
            got = swap(jnp.stack(later), "blk", bit)
    term = add(kept, other)
    bits = [("dom", bit) for bit in bits_of(peers)]
    bits[-1:-1] = [("blk", bit) for bit in inner]
    fours = [bits[i : i + 2] for i in range(0, len(bits), 2)]
    for i, four in enumerate(fours):
        first, last = i == 0, i == len(fours) - 1
        if first:
            term, agg = lax.optimization_barrier((term, agg))
            (layer_out,) = call(output_kernel, [((rows, width), BF16)], [VMEM] * 2, 16 * MIB)(
                agg, weight
            )
        if last:
            (feature_grad,) = call(
                backward_kernel, [((rows, width), BF16)], [SMEM] + [VMEM] * 6, 16 * MIB
            )(send_live, keep[0], got, third, halo, sends, weight)
        others = [swap_bits(term, four[:1])]
        if len(four) == 2:
            others += [swap_bits(term, four[1:]), swap_bits(term, four)]
        if first:
            others, layer_out, third = lax.optimization_barrier((others, layer_out, third))
        if last:
            others, feature_grad = lax.optimization_barrier((others, feature_grad))
        wide = [value.astype(F32) for value in (term, *others)]
        total = wide[0] + wide[1]
        if len(four) == 2:
            total += wide[2] + wide[3]
        term = total.astype(BF16)
    other = swap(term, "blk", 1)
    scale = float(groups * peers * rows) ** (-0.5)
    low = jnp.where(me % 2 == 0, term, other)
    high = jnp.where(me % 2 == 0, other, term)
    weight_grad = jnp.concatenate([low, high]).astype(F32) * scale
    return layer_out[None], feature_grad[None], weight_grad


def solution(mesh):
    return jax.shard_map(
        on_device,
        mesh=mesh,
        in_specs=(
            P("dom", "blk", None),
            P(),
            P("dom", "blk", None, None, None, None),
            P("dom", "blk", None, None),
            P("dom", "blk", None),
            P("dom", "blk", None, None),
            P("dom", "blk", None),
            P("dom", "blk", None, None),
            P("dom", "blk", None, None),
            P("dom", "blk", None),
        ),
        out_specs=(P("dom", "blk", None), P("dom", "blk", None), P()),
        check_vma=False,
    )
```

```python
import functools
import jax
import jax.numpy as jnp
from jax import lax
from jax.experimental import pallas as pl
from jax.experimental.pallas import tpu as pltpu
from jax.sharding import PartitionSpec as P

BF16 = jnp.bfloat16
F32 = jnp.float32
VMEM = pl.BlockSpec(memory_space=pltpu.VMEM)
SMEM = pl.BlockSpec(memory_space=pltpu.SMEM)
HBM = pl.BlockSpec(memory_space=pl.ANY)
MIB = 1 << 20


def swap(value, axis, bit):
    return lax.ppermute(value, axis, [(i, i ^ bit) for i in range(lax.axis_size(axis))])


def swap_bits(value, bits):
    groups, peers = lax.axis_size("blk"), lax.axis_size("dom")
    b_bits = sum(bit for axis, bit in bits if axis == "blk")
    d_bits = sum(bit for axis, bit in bits if axis == "dom")
    pairs = [
        (b * peers + d, (b ^ b_bits) * peers + (d ^ d_bits))
        for b in range(groups)
        for d in range(peers)
    ]
    return lax.ppermute(value, ("blk", "dom"), pairs)


def bits_of(size):
    return [1 << k for k in range(size.bit_length() - 1)]


def matmul(left, right, left_dim, right_dim):
    return lax.dot_general(
        left, right, (((left_dim,), (right_dim,)), ((), ())), preferred_element_type=F32
    )


def one_hot(rows, index):
    return lax.broadcasted_iota(jnp.int32, (rows, index.shape[1]), 0) == index


def flat(rows):
    return jnp.concatenate([rows[q : q + 1, :] for q in range(rows.shape[0])], axis=1)


def send_index_of(send_list, send_count):
    peers, slots = send_list.shape
    peer = lax.broadcasted_iota(jnp.int32, (peers, slots), 0)
    slot = lax.broadcasted_iota(jnp.int32, (peers, slots), 1)
    count = jnp.zeros((peers, slots), jnp.int32)
    for q in range(peers):
        count = jnp.where(peer == q, send_count[q], count)
    return flat(jnp.where(slot < count, send_list[...], -1))


def fetch(pairs, sems):
    copies = [pltpu.make_async_copy(src, dst, sems.at[i]) for i, (src, dst) in enumerate(pairs)]
    for copy in copies:
        copy.start()
    return copies


def halo_kernel(feats_in, grad_in, send_in, count_in, owner_in, edge_in, out, *scratch):
    feats, grad, send, count, owner, edge, sems = scratch
    sources = (feats_in, grad_in, send_in, count_in, owner_in, edge_in)
    for copy in fetch(list(zip(sources, scratch)), sems):
        copy.wait()
    rows, width = feats.shape
    peers, both, unused = out.shape
    slots = both // 2
    pick = one_hot(rows, send_index_of(send, count)).astype(BF16)
    sent = matmul(pick, feats[...], 0, 0)
    out[:, :slots, :] = sent.astype(BF16).reshape(peers, slots, width)
    back = matmul(weights_of(rows, owner, edge), grad[...], 0, 0)
    out[:, slots:, :] = back.astype(BF16).reshape(peers, slots, width)


def split_halves(blk, term, kept, sent):
    half = term.shape[0] // 2
    core = blk[0] % 2
    kept[...] = term[pl.ds(pl.multiple_of(core * half, half), half), :].astype(BF16)
    sent[...] = term[pl.ds(pl.multiple_of((1 - core) * half, half), half), :].astype(BF16)


def adjacency_kernel(groups, blk, pos_in, count_in, tiles_in, grad_in, *refs):
    panels_in, refs = refs[:groups], refs[groups:]
    (local, kept, sent, send, *keep), refs = refs[: 4 + groups // 2], refs[4 + groups // 2 :]
    dense, term, sems, *homes = refs
    pos, count, tiles, grad, *panels = homes
    unused, slots, tile, unused = tiles.shape
    rows, width = grad.shape
    per = rows // tile
    order = [blk[0] ^ j for j in range(groups)]
    few = fetch([(pos_in, pos), (count_in, count), (grad_in, grad)], sems)
    blocks = fetch([(tiles_in, tiles)], sems.at[pl.ds(3, 1)])
    others = fetch(list(zip(panels_in, panels)), sems.at[pl.ds(4, groups)])
    dense[...] = jnp.zeros_like(dense)
    for copy in few:
        copy.wait()
    for copy in blocks:
        copy.wait()
    for j, c in enumerate(order):
        for t in range(slots):
            spot = pos[c, t]
            row = pl.multiple_of((spot // per) * tile, tile)
            column = pl.multiple_of(j * rows + (spot % per) * tile, tile)
            live = t < count[c]
            dense[pl.ds(row, tile), pl.ds(column, tile)] = jnp.where(
                live, tiles[c, t], jnp.zeros((), BF16)
            )
    for copy in others:
        copy.wait()
    turned = grad[...].T
    for j in range(groups):
        part = matmul(turned, dense[:, j * rows : (j + 1) * rows], 1, 0).astype(BF16)
        if j % 2:
            send[j // 2] = part
        else:
            keep[j // 2][...] = part
    value = matmul(dense[:, :rows], panels[0][...], 1, 0)
    for j in range(1, groups):
        value += matmul(dense[:, j * rows : (j + 1) * rows], panels[j][...], 1, 0)
    rounded = value.astype(BF16)
    local[...] = rounded
    term[...] = matmul(rounded, grad[...], 0, 0)
    split_halves(blk, term, kept, sent)


def weights_of(rows, owner, edge):
    return jnp.where(one_hot(rows, flat(owner)), flat(edge), 0.0).astype(BF16)


def halo_sum(halo, owner, edge, rows):
    peers, both, width = halo.shape
    received = halo[:, : both // 2, :].reshape(-1, width)
    return matmul(weights_of(rows, owner, edge), received, 1, 0)


def halo_term_kernel(blk, halo, owner, edge, grad, kept, sent, term):
    rows, width = grad.shape
    term[...] = matmul(halo_sum(halo, owner, edge, rows).astype(BF16), grad[...], 0, 0)
    split_halves(blk, term, kept, sent)


def output_kernel(local, halo, owner, edge, weight, out):
    rows, width = out.shape
    total = local[...].astype(F32) + halo_sum(halo, owner, edge, rows)
    out[...] = matmul(total.astype(BF16), weight[...], 1, 0).astype(BF16)


def backward_kernel(send_count, first, others, third, halo, send_list, weight, out):
    rows, width = out.shape
    slots = halo.shape[1] // 2
    local = first[...].astype(F32) + others[0].astype(F32) + third[...].astype(F32)
    total = local.T + matmul(
        one_hot(rows, send_index_of(send_list, send_count)).astype(BF16),
        halo[:, slots:, :].reshape(-1, width),
        1,
        0,
    )
    out[...] = matmul(total.astype(BF16), weight[...], 1, 1).astype(BF16)


def call(kernel, outs, specs, limit, scratch=(), flops=1):
    return pl.pallas_call(
        kernel,
        out_shape=[jax.ShapeDtypeStruct(shape, dtype) for shape, dtype in outs],
        in_specs=specs,
        out_specs=[VMEM] * len(outs),
        scratch_shapes=list(scratch),
        cost_estimate=pl.CostEstimate(flops=flops, bytes_accessed=1, transcendentals=0),
        compiler_params=pltpu.CompilerParams(vmem_limit_bytes=limit),
    )


def add(*values):
    return sum(value.astype(F32) for value in values).astype(BF16)


def on_device(
    features,
    weight,
    tiles,
    tile_pos,
    tile_count,
    send_list,
    send_count,
    owner_map,
    halo_weight,
    cotangent,
):
    groups, peers = lax.axis_size("blk"), lax.axis_size("dom")
    feats, grad = features[0], cotangent[0]
    rows, width = feats.shape
    slots = send_list.shape[-1]
    links = peers * slots
    me = lax.axis_index("blk").astype(jnp.int32)
    blk = me.reshape(1)
    sends, send_live = send_list[0, 0], send_count[0, 0]
    owner, edge = owner_map[0, 0], halo_weight[0, 0]

    feats_far = swap(feats, "blk", groups // 2)
    (outgoing,) = call(
        halo_kernel,
        [((peers, 2 * slots, width), BF16)],
        [HBM] * 6,
        64 * MIB,
        [
            pltpu.VMEM((rows, width), BF16),
            pltpu.VMEM((rows, width), BF16),
            pltpu.VMEM((peers, slots), jnp.int32),
            pltpu.SMEM((peers,), jnp.int32),
            pltpu.VMEM((peers, slots), jnp.int32),
            pltpu.VMEM((peers, slots), F32),
            pltpu.SemaphoreType.DMA((6,)),
        ],
    )(feats, grad, sends, send_live, owner, edge)
    outgoing, near, tile_set = lax.optimization_barrier((outgoing, feats, tiles[0, 0]))
    halo = lax.all_to_all(outgoing, "dom", split_axis=0, concat_axis=0, tiled=True)

    panels = {0: near, groups // 2: feats_far}
    for bit in reversed(bits_of(groups // 2)):
        for j in list(panels):
            panels[j ^ bit] = swap(panels[j], "blk", bit)

    half = groups // 2
    panel = pltpu.VMEM((rows, width), BF16)
    half_term = ((width // 2, width), BF16)
    local, kept, sent, send, *keep = call(
        functools.partial(adjacency_kernel, groups),
        [((rows, width), BF16), half_term, half_term, ((half, width, rows), BF16)]
        + [((width, rows), BF16)] * half,
        [SMEM] + [HBM] * (4 + groups),
        61 * MIB,
        [
            pltpu.VMEM((rows, groups * rows), BF16),
            pltpu.VMEM((width, width), F32),
            pltpu.SemaphoreType.DMA((4 + groups,)),
            pltpu.SMEM(tile_pos.shape[2:], jnp.int32),
            pltpu.SMEM(tile_count.shape[2:], jnp.int32),
            pltpu.VMEM(tiles.shape[2:], BF16),
        ]
        + [panel] * (1 + groups),
    )(
        blk,
        tile_pos[0, 0],
        tile_count[0, 0],
        tile_set,
        grad,
        *[panels[j] for j in range(groups)],
    )
    got = swap(send, "blk", 1)

    near_term = (kept, swap(sent, "blk", 1))
    kept, sent = call(
        halo_term_kernel,
        [half_term, half_term],
        [SMEM] + [VMEM] * 4,
        16 * MIB,
        [pltpu.VMEM((width, width), F32)],
        flops=2 * 10**10,
    )(blk, halo, owner, edge, grad)
    other = swap(sent, "blk", 1)
    inner = bits_of(groups)[1:]
    for bit in inner:
        later = [add(keep[j], got[j]) for j in range(1, len(keep), 2)]
        if len(keep) == 2:
            third = swap(later[0], "blk", bit)
        else:
            keep = [add(keep[j], got[j]) for j in range(0, len(keep), 2)]
            got = swap(jnp.stack(later), "blk", bit)
    term = add(*near_term, kept, other)
    bits = [("dom", bit) for bit in bits_of(peers)]
    bits[-1:-1] = [("blk", bit) for bit in inner]
    fours = [bits[i : i + 2] for i in range(0, len(bits), 2)]
    for i, four in enumerate(fours):
        first, last = i == 0, i == len(fours) - 1
        if first:
            term, local = lax.optimization_barrier((term, local))
            (layer_out,) = call(output_kernel, [((rows, width), BF16)], [VMEM] * 5, 16 * MIB)(
                local, halo, owner, edge, weight
            )
        if last:
            (feature_grad,) = call(
                backward_kernel, [((rows, width), BF16)], [SMEM] + [VMEM] * 6, 16 * MIB
            )(send_live, keep[0], got, third, halo, sends, weight)
        ways = [four[1:], four, four[:1]] if len(four) == 2 else [four]
        others = [swap_bits(term, way) for way in ways]
        if first:
            others, layer_out, third = lax.optimization_barrier((others, layer_out, third))
        if last:
            others, feature_grad = lax.optimization_barrier((others, feature_grad))
        others = others[-1:] + others[:-1]
        wide = [value.astype(F32) for value in (term, *others)]
        total = wide[0] + wide[1]
        if len(four) == 2:
            total += wide[2] + wide[3]
        term = total.astype(BF16)
    other = swap(term, "blk", 1)
    scale = float(groups * peers * rows) ** (-0.5)
    low = jnp.where(me % 2 == 0, term, other)
    high = jnp.where(me % 2 == 0, other, term)
    weight_grad = jnp.concatenate([low, high]).astype(F32) * scale
    return layer_out[None], feature_grad[None], weight_grad


def solution(mesh):
    return jax.shard_map(
        on_device,
        mesh=mesh,
        in_specs=(
            P("dom", "blk", None),
            P(),
            P("dom", "blk", None, None, None, None),
            P("dom", "blk", None, None),
            P("dom", "blk", None),
            P("dom", "blk", None, None),
            P("dom", "blk", None),
            P("dom", "blk", None, None),
            P("dom", "blk", None, None),
            P("dom", "blk", None),
        ),
        out_specs=(P("dom", "blk", None), P("dom", "blk", None), P()),
        check_vma=False,
    )
```

```python
import functools
import jax
import jax.numpy as jnp
from jax import lax
from jax.experimental import pallas as pl
from jax.experimental.pallas import tpu as pltpu
from jax.sharding import PartitionSpec as P

BF16 = jnp.bfloat16
F32 = jnp.float32
VMEM = pl.BlockSpec(memory_space=pltpu.VMEM)
SMEM = pl.BlockSpec(memory_space=pltpu.SMEM)
HBM = pl.BlockSpec(memory_space=pl.ANY)
MIB = 1 << 20


def swap(value, axis, bit):
    return lax.ppermute(value, axis, [(i, i ^ bit) for i in range(lax.axis_size(axis))])


def swap_bits(value, even, odd):
    groups, peers = lax.axis_size("blk"), lax.axis_size("dom")
    pairs = []
    for b in range(groups):
        bits = odd if b % 2 else even
        b_bits = sum(bit for axis, bit in bits if axis == "blk")
        d_bits = sum(bit for axis, bit in bits if axis == "dom")
        pairs += [(b * peers + d, (b ^ b_bits) * peers + (d ^ d_bits)) for d in range(peers)]
    return lax.ppermute(value, ("blk", "dom"), pairs)


def bits_of(size):
    return [1 << k for k in range(size.bit_length() - 1)]


def matmul(left, right, left_dim, right_dim):
    return lax.dot_general(
        left, right, (((left_dim,), (right_dim,)), ((), ())), preferred_element_type=F32
    )


def one_hot(rows, index):
    return lax.broadcasted_iota(jnp.int32, (rows, index.shape[1]), 0) == index


def flat(rows):
    return jnp.concatenate([rows[q : q + 1, :] for q in range(rows.shape[0])], axis=1)


def send_index_of(send_list, send_count):
    peers, slots = send_list.shape
    peer = lax.broadcasted_iota(jnp.int32, (peers, slots), 0)
    slot = lax.broadcasted_iota(jnp.int32, (peers, slots), 1)
    count = jnp.zeros((peers, slots), jnp.int32)
    for q in range(peers):
        count = jnp.where(peer == q, send_count[q], count)
    return flat(jnp.where(slot < count, send_list[...], -1))


def fetch(pairs, sems):
    copies = [pltpu.make_async_copy(src, dst, sems.at[i]) for i, (src, dst) in enumerate(pairs)]
    for copy in copies:
        copy.start()
    return copies


def halo_kernel(feats_in, grad_in, send_in, count_in, owner_in, edge_in, out, *scratch):
    feats, grad, send, count, owner, edge, sems = scratch
    sources = (feats_in, grad_in, send_in, count_in, owner_in, edge_in)
    for copy in fetch(list(zip(sources, scratch)), sems):
        copy.wait()
    rows, width = feats.shape
    peers, both, unused = out.shape
    slots = both // 2
    pick = one_hot(rows, send_index_of(send, count)).astype(BF16)
    sent = matmul(pick, feats[...], 0, 0)
    out[:, :slots, :] = sent.astype(BF16).reshape(peers, slots, width)
    back = matmul(weights_of(rows, owner, edge), grad[...], 0, 0)
    out[:, slots:, :] = back.astype(BF16).reshape(peers, slots, width)


def split_halves(blk, term, kept, sent):
    half = term.shape[0] // 2
    core = blk[0] % 2
    kept[...] = term[pl.ds(pl.multiple_of(core * half, half), half), :].astype(BF16)
    sent[...] = term[pl.ds(pl.multiple_of((1 - core) * half, half), half), :].astype(BF16)


def adjacency_kernel(groups, blk, spots, tiles, grad, *refs):
    panels, refs = refs[:groups], refs[groups:]
    (local, kept, sent, send, *keep), (dense, term) = refs[:-2], refs[-2:]
    unused, slots, tile, unused = tiles.shape
    rows, width = grad.shape
    dense[...] = jnp.zeros_like(dense)
    for j in range(groups):
        c = blk[0] ^ j
        for t in range(slots):
            row = pl.multiple_of(spots[0, c, t], tile)
            column = pl.multiple_of(j * rows + spots[1, c, t], tile)
            dense[pl.ds(row, tile), pl.ds(column, tile)] = tiles[c, t]
    turned = grad[...].T
    for j in range(groups):
        part = matmul(turned, dense[:, j * rows : (j + 1) * rows], 1, 0).astype(BF16)
        if j % 2:
            send[j // 2] = part
        else:
            keep[j // 2][...] = part
    value = matmul(dense[:, :rows], panels[0][...], 1, 0)
    for j in range(1, groups):
        value += matmul(dense[:, j * rows : (j + 1) * rows], panels[j][...], 1, 0)
    rounded = value.astype(BF16)
    local[...] = rounded
    term[...] = matmul(rounded, grad[...], 0, 0)
    split_halves(blk, term, kept, sent)


def weights_of(rows, owner, edge):
    return jnp.where(one_hot(rows, flat(owner)), flat(edge), 0.0).astype(BF16)


def halo_sum(halo, owner, edge, rows):
    peers, both, width = halo.shape
    received = halo[:, : both // 2, :].reshape(-1, width)
    return matmul(weights_of(rows, owner, edge), received, 1, 0)


def halo_term_kernel(blk, halo, owner, edge, grad, kept, sent, term):
    rows, width = grad.shape
    term[...] = matmul(halo_sum(halo, owner, edge, rows).astype(BF16), grad[...], 0, 0)
    split_halves(blk, term, kept, sent)


def output_kernel(local, halo, owner, edge, weight, out):
    rows, width = out.shape
    total = local[...].astype(F32) + halo_sum(halo, owner, edge, rows)
    out[...] = matmul(total.astype(BF16), weight[...], 1, 0).astype(BF16)


def backward_kernel(send_count, first, others, third, halo, send_list, weight, out):
    rows, width = out.shape
    slots = halo.shape[1] // 2
    local = first[...].astype(F32) + others[0].astype(F32) + third[...].astype(F32)
    total = local.T + matmul(
        one_hot(rows, send_index_of(send_list, send_count)).astype(BF16),
        halo[:, slots:, :].reshape(-1, width),
        1,
        0,
    )
    out[...] = matmul(total.astype(BF16), weight[...], 1, 1).astype(BF16)


def call(kernel, outs, specs, limit, scratch=(), flops=1):
    return pl.pallas_call(
        kernel,
        out_shape=[jax.ShapeDtypeStruct(shape, dtype) for shape, dtype in outs],
        in_specs=specs,
        out_specs=[VMEM] * len(outs),
        scratch_shapes=list(scratch),
        cost_estimate=pl.CostEstimate(flops=flops, bytes_accessed=1, transcendentals=0),
        compiler_params=pltpu.CompilerParams(vmem_limit_bytes=limit),
    )


def add(*values):
    return sum(value.astype(F32) for value in values).astype(BF16)


def on_device(
    features,
    weight,
    tiles,
    tile_pos,
    tile_count,
    send_list,
    send_count,
    owner_map,
    halo_weight,
    cotangent,
):
    groups, peers = lax.axis_size("blk"), lax.axis_size("dom")
    feats, grad = features[0], cotangent[0]
    rows, width = feats.shape
    slots = send_list.shape[-1]
    links = peers * slots
    me = lax.axis_index("blk").astype(jnp.int32)
    blk = me.reshape(1)
    sends, send_live = send_list[0, 0], send_count[0, 0]
    owner, edge = owner_map[0, 0], halo_weight[0, 0]

    feats_far = swap(feats, "blk", groups // 2)
    (outgoing,) = call(
        halo_kernel,
        [((peers, 2 * slots, width), BF16)],
        [HBM] * 6,
        64 * MIB,
        [
            pltpu.VMEM((rows, width), BF16),
            pltpu.VMEM((rows, width), BF16),
            pltpu.VMEM((peers, slots), jnp.int32),
            pltpu.SMEM((peers,), jnp.int32),
            pltpu.VMEM((peers, slots), jnp.int32),
            pltpu.VMEM((peers, slots), F32),
            pltpu.SemaphoreType.DMA((6,)),
        ],
    )(feats, grad, sends, send_live, owner, edge)
    outgoing, near, tile_set, place = lax.optimization_barrier(
        (outgoing, feats, tiles[0, 0], tile_pos[0, 0])
    )
    halo = lax.all_to_all(outgoing, "dom", split_axis=0, concat_axis=0, tiled=True)

    near, feats_far = lax.optimization_barrier((near, feats_far))
    panels = {0: near, groups // 2: feats_far}
    for bit in reversed(bits_of(groups // 2)):
        for j in list(panels):
            panels[j ^ bit] = swap(panels[j], "blk", bit)

    half = groups // 2
    half_term = ((width // 2, width), BF16)
    tile = tiles.shape[-1]
    per = rows // tile
    live = jnp.arange(tiles.shape[3])[None, :] < tile_count[0, 0][:, None]
    live_tiles = jnp.where(live[..., None, None], tile_set, jnp.zeros((), BF16))
    spots = jnp.stack([place // per, place % per]) * tile
    local, kept, sent, send, *keep = call(
        functools.partial(adjacency_kernel, groups),
        [((rows, width), BF16), half_term, half_term, ((half, width, rows), BF16)]
        + [((width, rows), BF16)] * half,
        [SMEM] * 2 + [VMEM] * (2 + groups),
        40 * MIB,
        [pltpu.VMEM((rows, groups * rows), BF16), pltpu.VMEM((width, width), F32)],
    )(blk, spots, live_tiles, grad, *[panels[j] for j in range(groups)])
    got = swap(send, "blk", 1)

    near_term = (kept, swap(sent, "blk", 1))
    kept, sent = call(
        halo_term_kernel,
        [half_term, half_term],
        [SMEM] + [VMEM] * 4,
        16 * MIB,
        [pltpu.VMEM((width, width), F32)],
        flops=2 * 10**10,
    )(blk, halo, owner, edge, grad)
    other = swap(sent, "blk", 1)
    inner = bits_of(groups)[1:]
    for bit in inner:
        later = [add(keep[j], got[j]) for j in range(1, len(keep), 2)]
        if bit == inner[0]:
            other, later[0] = lax.optimization_barrier((other, later[0]))
        if len(keep) == 2:
            third = swap(later[0], "blk", bit)
        else:
            keep = [add(keep[j], got[j]) for j in range(0, len(keep), 2)]
            got = swap(jnp.stack(later), "blk", bit)
    term = add(*near_term, kept, other)
    bits = [("dom", bit) for bit in bits_of(peers)]
    bits[-1:-1] = [("blk", bit) for bit in inner]
    fours = [bits[i : i + 2] for i in range(0, len(bits), 2)]
    for i, four in enumerate(fours):
        first, last = i == 0, i == len(fours) - 1
        if first:
            term, local = lax.optimization_barrier((term, local))
            (layer_out,) = call(
                output_kernel, [((rows, width), BF16)], [VMEM] * 5, 16 * MIB, flops=2 * 10**10
            )(local, halo, owner, edge, weight)
        if last:
            (feature_grad,) = call(
                backward_kernel, [((rows, width), BF16)], [SMEM] + [VMEM] * 6, 16 * MIB
            )(send_live, keep[0], got, third, halo, sends, weight)
        mate = fours[i ^ 1] if i ^ 1 < len(fours) and len(fours[i ^ 1]) == len(four) else four
        ways = [slice(1, 2), slice(0, 2), slice(0, 1)] if len(four) == 2 else [slice(0, 1)]
        others = [swap_bits(term, four[way], mate[way]) for way in ways]
        if first:
            others, layer_out = lax.optimization_barrier((others, layer_out))
        if last:
            others, feature_grad = lax.optimization_barrier((others, feature_grad))
        others = others[-1:] + others[:-1]
        wide = [value.astype(F32) for value in (term, *others)]
        total = wide[0] + wide[1]
        if len(four) == 2:
            total += wide[2] + wide[3]
        term = total.astype(BF16)
    other = swap(term, "blk", 1)
    scale = float(groups * peers * rows) ** (-0.5)
    low = jnp.where(me % 2 == 0, term, other)
    high = jnp.where(me % 2 == 0, other, term)
    weight_grad = jnp.concatenate([low, high]).astype(F32) * scale
    return layer_out[None], feature_grad[None], weight_grad


def solution(mesh):
    return jax.shard_map(
        on_device,
        mesh=mesh,
        in_specs=(
            P("dom", "blk", None),
            P(),
            P("dom", "blk", None, None, None, None),
            P("dom", "blk", None, None),
            P("dom", "blk", None),
            P("dom", "blk", None, None),
            P("dom", "blk", None),
            P("dom", "blk", None, None),
            P("dom", "blk", None, None),
            P("dom", "blk", None),
        ),
        out_specs=(P("dom", "blk", None), P("dom", "blk", None), P()),
        check_vma=False,
    )
```

```python
import functools
import jax
import jax.numpy as jnp
from jax import lax
from jax.experimental import pallas as pl
from jax.experimental.pallas import tpu as pltpu
from jax.sharding import PartitionSpec as P

BF16 = jnp.bfloat16
F32 = jnp.float32
VMEM = pl.BlockSpec(memory_space=pltpu.VMEM)
SMEM = pl.BlockSpec(memory_space=pltpu.SMEM)
HBM = pl.BlockSpec(memory_space=pl.ANY)
MIB = 1 << 20


def swap(value, axis, bit):
    return lax.ppermute(value, axis, [(i, i ^ bit) for i in range(lax.axis_size(axis))])


def swap_bits(value, even, odd):
    groups, peers = lax.axis_size("blk"), lax.axis_size("dom")
    pairs = []
    for b in range(groups):
        bits = odd if b % 2 else even
        b_bits = sum(bit for axis, bit in bits if axis == "blk")
        d_bits = sum(bit for axis, bit in bits if axis == "dom")
        pairs += [(b * peers + d, (b ^ b_bits) * peers + (d ^ d_bits)) for d in range(peers)]
    return lax.ppermute(value, ("blk", "dom"), pairs)


def bits_of(size):
    return [1 << k for k in range(size.bit_length() - 1)]


def matmul(left, right, left_dim, right_dim):
    return lax.dot_general(
        left, right, (((left_dim,), (right_dim,)), ((), ())), preferred_element_type=F32
    )


def one_hot(rows, index):
    return lax.broadcasted_iota(jnp.int32, (rows, index.shape[1]), 0) == index


def flat(rows):
    return jnp.concatenate([rows[q : q + 1, :] for q in range(rows.shape[0])], axis=1)


def send_index_of(send_list, send_count):
    peers, slots = send_list.shape
    peer = lax.broadcasted_iota(jnp.int32, (peers, slots), 0)
    slot = lax.broadcasted_iota(jnp.int32, (peers, slots), 1)
    count = jnp.zeros((peers, slots), jnp.int32)
    for q in range(peers):
        count = jnp.where(peer == q, send_count[q], count)
    return flat(jnp.where(slot < count, send_list[...], -1))


def fetch(pairs, sems):
    copies = [pltpu.make_async_copy(src, dst, sems.at[i]) for i, (src, dst) in enumerate(pairs)]
    for copy in copies:
        copy.start()
    return copies


def halo_kernel(feats_in, grad_in, send_in, count_in, owner_in, edge_in, out, *scratch):
    feats, grad, send, count, owner, edge, sems = scratch
    sources = (feats_in, grad_in, send_in, count_in, owner_in, edge_in)
    for copy in fetch(list(zip(sources, scratch)), sems):
        copy.wait()
    rows, width = feats.shape
    peers, both, unused = out.shape
    slots = both // 2
    pick = one_hot(rows, send_index_of(send, count)).astype(BF16)
    sent = matmul(pick, feats[...], 0, 0)
    out[:, :slots, :] = sent.astype(BF16).reshape(peers, slots, width)
    back = matmul(weights_of(rows, owner, edge), grad[...], 0, 0)
    out[:, slots:, :] = back.astype(BF16).reshape(peers, slots, width)


def split_halves(blk, term, kept, sent):
    half = term.shape[0] // 2
    core = blk[0] % 2
    kept[...] = term[pl.ds(pl.multiple_of(core * half, half), half), :].astype(BF16)
    sent[...] = term[pl.ds(pl.multiple_of((1 - core) * half, half), half), :].astype(BF16)


def adjacency_kernel(groups, blk, spots, tiles, grad, *refs):
    panels, refs = refs[:groups], refs[groups:]
    (local, kept, sent, send, *keep), (dense, term) = refs[:-2], refs[-2:]
    unused, slots, tile, unused = tiles.shape
    rows, width = grad.shape
    dense[...] = jnp.zeros_like(dense)
    for j in range(groups):
        c = blk[0] ^ j
        for t in range(slots):
            row = pl.multiple_of(spots[0, c, t], tile)
            column = pl.multiple_of(j * rows + spots[1, c, t], tile)
            dense[pl.ds(row, tile), pl.ds(column, tile)] = tiles[c, t]
    turned = grad[...].T
    for j in range(groups):
        part = matmul(turned, dense[:, j * rows : (j + 1) * rows], 1, 0).astype(BF16)
        if j % 2:
            send[j // 2] = part
        else:
            keep[j // 2][...] = part
    value = matmul(dense[:, :rows], panels[0][...], 1, 0)
    for j in range(1, groups):
        value += matmul(dense[:, j * rows : (j + 1) * rows], panels[j][...], 1, 0)
    rounded = value.astype(BF16)
    local[...] = rounded
    term[...] = matmul(rounded, grad[...], 0, 0)
    split_halves(blk, term, kept, sent)


def weights_of(rows, owner, edge):
    return jnp.where(one_hot(rows, flat(owner)), flat(edge), 0.0).astype(BF16)


def halo_sum(halo, owner, edge, rows):
    peers, both, width = halo.shape
    received = halo[:, : both // 2, :].reshape(-1, width)
    return matmul(weights_of(rows, owner, edge), received, 1, 0)


def halo_term_kernel(blk, halo, owner, edge, grad, kept, sent, term):
    rows, width = grad.shape
    term[...] = matmul(halo_sum(halo, owner, edge, rows).astype(BF16), grad[...], 0, 0)
    split_halves(blk, term, kept, sent)


def output_kernel(local, halo, owner, edge, weight, out):
    rows, width = out.shape
    total = local[...].astype(F32) + halo_sum(halo, owner, edge, rows)
    out[...] = matmul(total.astype(BF16), weight[...], 1, 0).astype(BF16)


def backward_kernel(send_count, first, others, third, halo, send_list, weight, out):
    rows, width = out.shape
    slots = halo.shape[1] // 2
    local = first[...].astype(F32) + others[0].astype(F32) + third[...].astype(F32)
    total = local.T + matmul(
        one_hot(rows, send_index_of(send_list, send_count)).astype(BF16),
        halo[:, slots:, :].reshape(-1, width),
        1,
        0,
    )
    out[...] = matmul(total.astype(BF16), weight[...], 1, 1).astype(BF16)


def call(kernel, outs, specs, limit, scratch=(), flops=1):
    return pl.pallas_call(
        kernel,
        out_shape=[jax.ShapeDtypeStruct(shape, dtype) for shape, dtype in outs],
        in_specs=specs,
        out_specs=[VMEM] * len(outs),
        scratch_shapes=list(scratch),
        cost_estimate=pl.CostEstimate(flops=flops, bytes_accessed=1, transcendentals=0),
        compiler_params=pltpu.CompilerParams(vmem_limit_bytes=limit),
    )


def add(*values):
    return sum(value.astype(F32) for value in values).astype(BF16)


def on_device(
    features,
    weight,
    tiles,
    tile_pos,
    tile_count,
    send_list,
    send_count,
    owner_map,
    halo_weight,
    cotangent,
):
    groups, peers = lax.axis_size("blk"), lax.axis_size("dom")
    feats, grad = features[0], cotangent[0]
    rows, width = feats.shape
    slots = send_list.shape[-1]
    links = peers * slots
    me = lax.axis_index("blk").astype(jnp.int32)
    blk = me.reshape(1)
    sends, send_live = send_list[0, 0], send_count[0, 0]
    owner, edge = owner_map[0, 0], halo_weight[0, 0]

    feats_far = swap(feats, "blk", groups // 2)
    (outgoing,) = call(
        halo_kernel,
        [((peers, 2 * slots, width), BF16)],
        [HBM] * 6,
        64 * MIB,
        [
            pltpu.VMEM((rows, width), BF16),
            pltpu.VMEM((rows, width), BF16),
            pltpu.VMEM((peers, slots), jnp.int32),
            pltpu.SMEM((peers,), jnp.int32),
            pltpu.VMEM((peers, slots), jnp.int32),
            pltpu.VMEM((peers, slots), F32),
            pltpu.SemaphoreType.DMA((6,)),
        ],
    )(feats, grad, sends, send_live, owner, edge)
    outgoing, near, tile_set, place = lax.optimization_barrier(
        (outgoing, feats, tiles[0, 0], tile_pos[0, 0])
    )
    halo = lax.all_to_all(outgoing, "dom", split_axis=0, concat_axis=0, tiled=True)

    near, feats_far = lax.optimization_barrier((near, feats_far))
    panels = {0: near, groups // 2: feats_far}
    for bit in reversed(bits_of(groups // 2)):
        for j in list(panels):
            panels[j ^ bit] = swap(panels[j], "blk", bit)

    half = groups // 2
    half_term = ((width // 2, width), BF16)
    tile = tiles.shape[-1]
    per = rows // tile
    live = jnp.arange(tiles.shape[3])[None, :] < tile_count[0, 0][:, None]
    live_tiles = jnp.where(live[..., None, None], tile_set, jnp.zeros((), BF16))
    spots = jnp.stack([place // per, place % per]) * tile
    local, kept, sent, send, *keep = call(
        functools.partial(adjacency_kernel, groups),
        [((rows, width), BF16), half_term, half_term, ((half, width, rows), BF16)]
        + [((width, rows), BF16)] * half,
        [SMEM] * 2 + [VMEM] * (2 + groups),
        40 * MIB,
        [pltpu.VMEM((rows, groups * rows), BF16), pltpu.VMEM((width, width), F32)],
    )(blk, spots, live_tiles, grad, *[panels[j] for j in range(groups)])
    got = swap(send, "blk", 1)

    near_term = (kept, swap(sent, "blk", 1))
    kept, sent = call(
        halo_term_kernel,
        [half_term, half_term],
        [SMEM] + [VMEM] * 4,
        16 * MIB,
        [pltpu.VMEM((width, width), F32)],
        flops=2 * 10**10,
    )(blk, halo, owner, edge, grad)
    other = swap(sent, "blk", 1)
    inner = bits_of(groups)[1:]
    for bit in inner:
        later = [add(keep[j], got[j]) for j in range(1, len(keep), 2)]
        if bit == inner[0]:
            other, later[0] = lax.optimization_barrier((other, later[0]))
        if len(keep) == 2:
            third = swap(later[0], "blk", bit)
        else:
            keep = [add(keep[j], got[j]) for j in range(0, len(keep), 2)]
            got = swap(jnp.stack(later), "blk", bit)
    term = add(*near_term, kept, other)
    bits = [("dom", bit) for bit in bits_of(peers)]
    bits = bits[1:] + bits[:1] + [("blk", bit) for bit in inner]
    fours = [bits[i : i + 2] for i in range(0, len(bits), 2)]
    for i, four in enumerate(fours):
        first, last = i == 0, i == len(fours) - 1
        if first:
            term, local = lax.optimization_barrier((term, local))
            (layer_out,) = call(
                output_kernel, [((rows, width), BF16)], [VMEM] * 5, 16 * MIB, flops=2 * 10**10
            )(local, halo, owner, edge, weight)
        if last:
            (feature_grad,) = call(
                backward_kernel, [((rows, width), BF16)], [SMEM] + [VMEM] * 6, 16 * MIB
            )(send_live, keep[0], got, third, halo, sends, weight)
        mate = fours[i ^ 1] if i ^ 1 < len(fours) and len(fours[i ^ 1]) == len(four) else four
        ways = [slice(1, 2), slice(0, 2), slice(0, 1)] if len(four) == 2 else [slice(0, 1)]
        others = [swap_bits(term, four[way], mate[way]) for way in ways]
        if first:
            others, layer_out = lax.optimization_barrier((others, layer_out))
        if last:
            others, feature_grad = lax.optimization_barrier((others, feature_grad))
        others = others[-1:] + others[:-1]
        wide = [value.astype(F32) for value in (term, *others)]
        total = wide[0] + wide[1]
        if len(four) == 2:
            total += wide[2] + wide[3]
        term = total.astype(BF16)
    other = swap(term, "blk", 1)
    scale = float(groups * peers * rows) ** (-0.5)
    low = jnp.where(me % 2 == 0, term, other)
    high = jnp.where(me % 2 == 0, other, term)
    weight_grad = jnp.concatenate([low, high]).astype(F32) * scale
    return layer_out[None], feature_grad[None], weight_grad


def solution(mesh):
    return jax.shard_map(
        on_device,
        mesh=mesh,
        in_specs=(
            P("dom", "blk", None),
            P(),
            P("dom", "blk", None, None, None, None),
            P("dom", "blk", None, None),
            P("dom", "blk", None),
            P("dom", "blk", None, None),
            P("dom", "blk", None),
            P("dom", "blk", None, None),
            P("dom", "blk", None, None),
            P("dom", "blk", None),
        ),
        out_specs=(P("dom", "blk", None), P("dom", "blk", None), P()),
        check_vma=False,
    )
```

```python
import functools
import jax
import jax.numpy as jnp
from jax import lax
from jax.experimental import pallas as pl
from jax.experimental.pallas import tpu as pltpu
from jax.sharding import PartitionSpec as P

BF16 = jnp.bfloat16
F32 = jnp.float32
VMEM = pl.BlockSpec(memory_space=pltpu.VMEM)
SMEM = pl.BlockSpec(memory_space=pltpu.SMEM)
HBM = pl.BlockSpec(memory_space=pl.ANY)
MIB = 1 << 20


def swap(value, axis, bit):
    return lax.ppermute(value, axis, [(i, i ^ bit) for i in range(lax.axis_size(axis))])


def swap_bits(value, even, odd):
    groups, peers = lax.axis_size("blk"), lax.axis_size("dom")
    pairs = []
    for b in range(groups):
        bits = odd if b % 2 else even
        b_bits = sum(bit for axis, bit in bits if axis == "blk")
        d_bits = sum(bit for axis, bit in bits if axis == "dom")
        pairs += [(b * peers + d, (b ^ b_bits) * peers + (d ^ d_bits)) for d in range(peers)]
    return lax.ppermute(value, ("blk", "dom"), pairs)


def bits_of(size):
    return [1 << k for k in range(size.bit_length() - 1)]


def matmul(left, right, left_dim, right_dim):
    return lax.dot_general(
        left, right, (((left_dim,), (right_dim,)), ((), ())), preferred_element_type=F32
    )


def one_hot(rows, index):
    return lax.broadcasted_iota(jnp.int32, (rows, index.shape[1]), 0) == index


def flat(rows):
    return jnp.concatenate([rows[q : q + 1, :] for q in range(rows.shape[0])], axis=1)


def send_index_of(send_list, send_count):
    peers, slots = send_list.shape
    peer = lax.broadcasted_iota(jnp.int32, (peers, slots), 0)
    slot = lax.broadcasted_iota(jnp.int32, (peers, slots), 1)
    count = jnp.zeros((peers, slots), jnp.int32)
    for q in range(peers):
        count = jnp.where(peer == q, send_count[q], count)
    return flat(jnp.where(slot < count, send_list[...], -1))


def fetch(pairs, sems):
    copies = [pltpu.make_async_copy(src, dst, sems.at[i]) for i, (src, dst) in enumerate(pairs)]
    for copy in copies:
        copy.start()
    return copies


def halo_kernel(feats_in, grad_in, send_in, count_in, owner_in, edge_in, out, *scratch):
    feats, grad, send, count, owner, edge, sems = scratch
    sources = (feats_in, grad_in, send_in, count_in, owner_in, edge_in)
    for copy in fetch(list(zip(sources, scratch)), sems):
        copy.wait()
    rows, width = feats.shape
    peers, both, unused = out.shape
    slots = both // 2
    pick = one_hot(rows, send_index_of(send, count)).astype(BF16)
    sent = matmul(pick, feats[...], 0, 0)
    out[:, :slots, :] = sent.astype(BF16).reshape(peers, slots, width)
    back = matmul(weights_of(rows, owner, edge), grad[...], 0, 0)
    out[:, slots:, :] = back.astype(BF16).reshape(peers, slots, width)


def split_halves(blk, term, kept, sent):
    half = term.shape[0] // 2
    core = blk[0] % 2
    kept[...] = term[pl.ds(pl.multiple_of(core * half, half), half), :].astype(BF16)
    sent[...] = term[pl.ds(pl.multiple_of((1 - core) * half, half), half), :].astype(BF16)


def adjacency_kernel(groups, blk, spots, tiles, grad, *refs):
    panels, refs = refs[:groups], refs[groups:]
    (local, kept, sent, send, *keep), (dense, term) = refs[:-2], refs[-2:]
    unused, slots, tile, unused = tiles.shape
    rows, width = grad.shape
    dense[...] = jnp.zeros_like(dense)
    for j in range(groups):
        c = blk[0] ^ j
        for t in range(slots):
            row = pl.multiple_of(spots[0, c, t], tile)
            column = pl.multiple_of(j * rows + spots[1, c, t], tile)
            dense[pl.ds(row, tile), pl.ds(column, tile)] = tiles[c, t]
    turned = grad[...].T
    for j in range(groups):
        part = matmul(turned, dense[:, j * rows : (j + 1) * rows], 1, 0).astype(BF16)
        if j % 2:
            send[j // 2] = part
        else:
            keep[j // 2][...] = part
    value = matmul(dense[:, :rows], panels[0][...], 1, 0)
    for j in range(1, groups):
        value += matmul(dense[:, j * rows : (j + 1) * rows], panels[j][...], 1, 0)
    rounded = value.astype(BF16)
    local[...] = rounded
    term[...] = matmul(rounded, grad[...], 0, 0)
    split_halves(blk, term, kept, sent)


def weights_of(rows, owner, edge):
    return jnp.where(one_hot(rows, flat(owner)), flat(edge), 0.0).astype(BF16)


def halo_sum(halo, owner, edge, rows):
    peers, both, width = halo.shape
    received = halo[:, : both // 2, :].reshape(-1, width)
    return matmul(weights_of(rows, owner, edge), received, 1, 0)


def halo_term_kernel(blk, halo, outgoing, kept, sent, term):
    peers, both, width = halo.shape
    received = halo[:, : both // 2, :].reshape(-1, width)
    weighted = outgoing[:, both // 2 :, :].reshape(-1, width)
    term[...] = matmul(received, weighted, 0, 0)
    split_halves(blk, term, kept, sent)


def output_kernel(local, halo, owner, edge, weight, out):
    rows, width = out.shape
    total = local[...].astype(F32) + halo_sum(halo, owner, edge, rows)
    out[...] = matmul(total.astype(BF16), weight[...], 1, 0).astype(BF16)


def backward_kernel(send_count, first, others, third, halo, send_list, weight, out):
    rows, width = out.shape
    slots = halo.shape[1] // 2
    local = first[...].astype(F32) + others[0].astype(F32) + third[...].astype(F32)
    total = local.T + matmul(
        one_hot(rows, send_index_of(send_list, send_count)).astype(BF16),
        halo[:, slots:, :].reshape(-1, width),
        1,
        0,
    )
    out[...] = matmul(total.astype(BF16), weight[...], 1, 1).astype(BF16)


def call(kernel, outs, specs, limit, scratch=(), flops=1):
    return pl.pallas_call(
        kernel,
        out_shape=[jax.ShapeDtypeStruct(shape, dtype) for shape, dtype in outs],
        in_specs=specs,
        out_specs=[VMEM] * len(outs),
        scratch_shapes=list(scratch),
        cost_estimate=pl.CostEstimate(flops=flops, bytes_accessed=1, transcendentals=0),
        compiler_params=pltpu.CompilerParams(vmem_limit_bytes=limit),
    )


def add(*values):
    return sum(value.astype(F32) for value in values).astype(BF16)


def on_device(
    features,
    weight,
    tiles,
    tile_pos,
    tile_count,
    send_list,
    send_count,
    owner_map,
    halo_weight,
    cotangent,
):
    groups, peers = lax.axis_size("blk"), lax.axis_size("dom")
    feats, grad = features[0], cotangent[0]
    rows, width = feats.shape
    slots = send_list.shape[-1]
    links = peers * slots
    me = lax.axis_index("blk").astype(jnp.int32)
    blk = me.reshape(1)
    sends, send_live = send_list[0, 0], send_count[0, 0]
    owner, edge = owner_map[0, 0], halo_weight[0, 0]

    feats_far = swap(feats, "blk", groups // 2)
    (outgoing,) = call(
        halo_kernel,
        [((peers, 2 * slots, width), BF16)],
        [HBM] * 6,
        64 * MIB,
        [
            pltpu.VMEM((rows, width), BF16),
            pltpu.VMEM((rows, width), BF16),
            pltpu.VMEM((peers, slots), jnp.int32),
            pltpu.SMEM((peers,), jnp.int32),
            pltpu.VMEM((peers, slots), jnp.int32),
            pltpu.VMEM((peers, slots), F32),
            pltpu.SemaphoreType.DMA((6,)),
        ],
    )(feats, grad, sends, send_live, owner, edge)
    outgoing, near, tile_set, place = lax.optimization_barrier(
        (outgoing, feats, tiles[0, 0], tile_pos[0, 0])
    )
    halo = lax.all_to_all(outgoing, "dom", split_axis=0, concat_axis=0, tiled=True)

    near, feats_far = lax.optimization_barrier((near, feats_far))
    panels = {0: near, groups // 2: feats_far}
    for bit in reversed(bits_of(groups // 2)):
        for j in list(panels):
            panels[j ^ bit] = swap(panels[j], "blk", bit)

    half = groups // 2
    half_term = ((width // 2, width), BF16)
    tile = tiles.shape[-1]
    per = rows // tile
    live = jnp.arange(tiles.shape[3])[None, :] < tile_count[0, 0][:, None]
    live_tiles = jnp.where(live[..., None, None], tile_set, jnp.zeros((), BF16))
    spots = jnp.stack([place // per, place % per]) * tile
    local, kept, sent, send, *keep = call(
        functools.partial(adjacency_kernel, groups),
        [((rows, width), BF16), half_term, half_term, ((half, width, rows), BF16)]
        + [((width, rows), BF16)] * half,
        [SMEM] * 2 + [VMEM] * (2 + groups),
        40 * MIB,
        [pltpu.VMEM((rows, groups * rows), BF16), pltpu.VMEM((width, width), F32)],
    )(blk, spots, live_tiles, grad, *[panels[j] for j in range(groups)])
    got = swap(send, "blk", 1)

    near_term = (kept, swap(sent, "blk", 1))
    kept, sent = call(
        halo_term_kernel,
        [half_term, half_term],
        [SMEM] + [VMEM] * 2,
        16 * MIB,
        [pltpu.VMEM((width, width), F32)],
        flops=2 * 10**10,
    )(blk, halo, outgoing)
    other = swap(sent, "blk", 1)
    inner = bits_of(groups)[1:]
    for bit in inner:
        later = [add(keep[j], got[j]) for j in range(1, len(keep), 2)]
        if bit == inner[0]:
            other, later[0] = lax.optimization_barrier((other, later[0]))
        if len(keep) == 2:
            third = swap(later[0], "blk", bit)
        else:
            keep = [add(keep[j], got[j]) for j in range(0, len(keep), 2)]
            got = swap(jnp.stack(later), "blk", bit)
    term = add(*near_term, kept, other)
    bits = [("dom", bit) for bit in bits_of(peers)]
    bits = bits[1:] + bits[:1] + [("blk", bit) for bit in inner]
    fours = [bits[i : i + 2] for i in range(0, len(bits), 2)]
    for i, four in enumerate(fours):
        first, last = i == 0, i == len(fours) - 1
        if first:
            term, local = lax.optimization_barrier((term, local))
            (layer_out,) = call(
                output_kernel, [((rows, width), BF16)], [VMEM] * 5, 16 * MIB, flops=2 * 10**10
            )(local, halo, owner, edge, weight)
        if last:
            (feature_grad,) = call(
                backward_kernel, [((rows, width), BF16)], [SMEM] + [VMEM] * 6, 16 * MIB
            )(send_live, keep[0], got, third, halo, sends, weight)
        mate = fours[i ^ 1] if i ^ 1 < len(fours) and len(fours[i ^ 1]) == len(four) else four
        ways = [slice(1, 2), slice(0, 2), slice(0, 1)] if len(four) == 2 else [slice(0, 1)]
        others = [swap_bits(term, four[way], mate[way]) for way in ways]
        if first:
            others, layer_out = lax.optimization_barrier((others, layer_out))
        if last:
            others, feature_grad = lax.optimization_barrier((others, feature_grad))
        others = others[-1:] + others[:-1]
        wide = [value.astype(F32) for value in (term, *others)]
        total = wide[0] + wide[1]
        if len(four) == 2:
            total += wide[2] + wide[3]
        term = total.astype(BF16)
    other = swap(term, "blk", 1)
    scale = float(groups * peers * rows) ** (-0.5)
    low = jnp.where(me % 2 == 0, term, other)
    high = jnp.where(me % 2 == 0, other, term)
    weight_grad = jnp.concatenate([low, high]).astype(F32) * scale
    return layer_out[None], feature_grad[None], weight_grad


def solution(mesh):
    return jax.shard_map(
        on_device,
        mesh=mesh,
        in_specs=(
            P("dom", "blk", None),
            P(),
            P("dom", "blk", None, None, None, None),
            P("dom", "blk", None, None),
            P("dom", "blk", None),
            P("dom", "blk", None, None),
            P("dom", "blk", None),
            P("dom", "blk", None, None),
            P("dom", "blk", None, None),
            P("dom", "blk", None),
        ),
        out_specs=(P("dom", "blk", None), P("dom", "blk", None), P()),
        check_vma=False,
    )
```

```python
import functools
import jax
import jax.numpy as jnp
from jax import lax
from jax.experimental import pallas as pl
from jax.experimental.pallas import tpu as pltpu
from jax.sharding import PartitionSpec as P

BF16 = jnp.bfloat16
F32 = jnp.float32
VMEM = pl.BlockSpec(memory_space=pltpu.VMEM)
SMEM = pl.BlockSpec(memory_space=pltpu.SMEM)
HBM = pl.BlockSpec(memory_space=pl.ANY)
MIB = 1 << 20


def swap(value, axis, bit):
    return lax.ppermute(value, axis, [(i, i ^ bit) for i in range(lax.axis_size(axis))])


def swap_bits(value, even, odd):
    groups, peers = lax.axis_size("blk"), lax.axis_size("dom")
    pairs = []
    for b in range(groups):
        bits = odd if b % 2 else even
        b_bits = sum(bit for axis, bit in bits if axis == "blk")
        d_bits = sum(bit for axis, bit in bits if axis == "dom")
        pairs += [(b * peers + d, (b ^ b_bits) * peers + (d ^ d_bits)) for d in range(peers)]
    return lax.ppermute(value, ("blk", "dom"), pairs)


def bits_of(size):
    return [1 << k for k in range(size.bit_length() - 1)]


def matmul(left, right, left_dim, right_dim):
    return lax.dot_general(
        left, right, (((left_dim,), (right_dim,)), ((), ())), preferred_element_type=F32
    )


def one_hot(rows, index):
    return lax.broadcasted_iota(jnp.int32, (rows, index.shape[1]), 0) == index


def flat(rows):
    return jnp.concatenate([rows[q : q + 1, :] for q in range(rows.shape[0])], axis=1)


def send_index_of(send_list, send_count):
    peers, slots = send_list.shape
    peer = lax.broadcasted_iota(jnp.int32, (peers, slots), 0)
    slot = lax.broadcasted_iota(jnp.int32, (peers, slots), 1)
    count = jnp.zeros((peers, slots), jnp.int32)
    for q in range(peers):
        count = jnp.where(peer == q, send_count[q], count)
    return flat(jnp.where(slot < count, send_list[...], -1))


def fetch(pairs, sems):
    copies = [pltpu.make_async_copy(src, dst, sems.at[i]) for i, (src, dst) in enumerate(pairs)]
    for copy in copies:
        copy.start()
    return copies


def halo_kernel(feats_in, grad_in, send_in, count_in, owner_in, edge_in, out, *scratch):
    feats, grad, send, count, owner, edge, sems = scratch
    sources = (feats_in, grad_in, send_in, count_in, owner_in, edge_in)
    for copy in fetch(list(zip(sources, scratch)), sems):
        copy.wait()
    rows, width = feats.shape
    peers, both, unused = out.shape
    slots = both // 2
    pick = one_hot(rows, send_index_of(send, count)).astype(BF16)
    sent = matmul(pick, feats[...], 0, 0)
    out[:, :slots, :] = sent.astype(BF16).reshape(peers, slots, width)
    back = matmul(weights_of(rows, owner, edge), grad[...], 0, 0)
    out[:, slots:, :] = back.astype(BF16).reshape(peers, slots, width)


def split_halves(blk, term, kept, sent):
    half = term.shape[0] // 2
    core = blk[0] % 2
    kept[...] = term[pl.ds(pl.multiple_of(core * half, half), half), :].astype(BF16)
    sent[...] = term[pl.ds(pl.multiple_of((1 - core) * half, half), half), :].astype(BF16)


def adjacency_kernel(groups, blk, spots, tiles, grad, *refs):
    panels, refs = refs[:groups], refs[groups:]
    (local, term, send, *keep), dense = refs[:-1], refs[-1]
    unused, slots, tile, unused = tiles.shape
    rows, width = grad.shape
    dense[...] = jnp.zeros_like(dense)
    for j in range(groups):
        c = blk[0] ^ j
        for t in range(slots):
            row = pl.multiple_of(spots[0, c, t], tile)
            column = pl.multiple_of(j * rows + spots[1, c, t], tile)
            dense[pl.ds(row, tile), pl.ds(column, tile)] = tiles[c, t]
    turned = grad[...].T
    for j in range(groups):
        part = matmul(turned, dense[:, j * rows : (j + 1) * rows], 1, 0).astype(BF16)
        if j % 2:
            send[j // 2] = part
        else:
            keep[j // 2][...] = part
    value = matmul(dense[:, :rows], panels[0][...], 1, 0)
    for j in range(1, groups):
        value += matmul(dense[:, j * rows : (j + 1) * rows], panels[j][...], 1, 0)
    rounded = value.astype(BF16)
    local[...] = rounded
    term[...] = matmul(rounded, grad[...], 0, 0)


def weights_of(rows, owner, edge):
    return jnp.where(one_hot(rows, flat(owner)), flat(edge), 0.0).astype(BF16)


def halo_sum(halo, owner, edge, rows):
    peers, both, width = halo.shape
    received = halo[:, : both // 2, :].reshape(-1, width)
    return matmul(weights_of(rows, owner, edge), received, 1, 0)


def halo_term_kernel(blk, near, halo, outgoing, kept, sent, term):
    peers, both, width = halo.shape
    received = halo[:, : both // 2, :].reshape(-1, width)
    weighted = outgoing[:, both // 2 :, :].reshape(-1, width)
    term[...] = near[...] + matmul(received, weighted, 0, 0)
    split_halves(blk, term, kept, sent)


def output_kernel(local, halo, owner, edge, weight, out):
    rows, width = out.shape
    total = local[...].astype(F32) + halo_sum(halo, owner, edge, rows)
    out[...] = matmul(total.astype(BF16), weight[...], 1, 0).astype(BF16)


def backward_kernel(send_count, first, others, third, halo, send_list, weight, out):
    rows, width = out.shape
    slots = halo.shape[1] // 2
    local = first[...].astype(F32) + others[0].astype(F32) + third[...].astype(F32)
    total = local.T + matmul(
        one_hot(rows, send_index_of(send_list, send_count)).astype(BF16),
        halo[:, slots:, :].reshape(-1, width),
        1,
        0,
    )
    out[...] = matmul(total.astype(BF16), weight[...], 1, 1).astype(BF16)


def call(kernel, outs, specs, limit, scratch=(), flops=1):
    return pl.pallas_call(
        kernel,
        out_shape=[jax.ShapeDtypeStruct(shape, dtype) for shape, dtype in outs],
        in_specs=specs,
        out_specs=[VMEM] * len(outs),
        scratch_shapes=list(scratch),
        cost_estimate=pl.CostEstimate(flops=flops, bytes_accessed=1, transcendentals=0),
        compiler_params=pltpu.CompilerParams(vmem_limit_bytes=limit),
    )


def add(*values):
    return sum(value.astype(F32) for value in values).astype(BF16)


def on_device(
    features,
    weight,
    tiles,
    tile_pos,
    tile_count,
    send_list,
    send_count,
    owner_map,
    halo_weight,
    cotangent,
):
    groups, peers = lax.axis_size("blk"), lax.axis_size("dom")
    feats, grad = features[0], cotangent[0]
    rows, width = feats.shape
    slots = send_list.shape[-1]
    links = peers * slots
    me = lax.axis_index("blk").astype(jnp.int32)
    blk = me.reshape(1)
    sends, send_live = send_list[0, 0], send_count[0, 0]
    owner, edge = owner_map[0, 0], halo_weight[0, 0]

    feats_far = swap(feats, "blk", groups // 2)
    (outgoing,) = call(
        halo_kernel,
        [((peers, 2 * slots, width), BF16)],
        [HBM] * 6,
        64 * MIB,
        [
            pltpu.VMEM((rows, width), BF16),
            pltpu.VMEM((rows, width), BF16),
            pltpu.VMEM((peers, slots), jnp.int32),
            pltpu.SMEM((peers,), jnp.int32),
            pltpu.VMEM((peers, slots), jnp.int32),
            pltpu.VMEM((peers, slots), F32),
            pltpu.SemaphoreType.DMA((6,)),
        ],
    )(feats, grad, sends, send_live, owner, edge)
    outgoing, near, tile_set, place = lax.optimization_barrier(
        (outgoing, feats, tiles[0, 0], tile_pos[0, 0])
    )
    halo = lax.all_to_all(outgoing, "dom", split_axis=0, concat_axis=0, tiled=True)

    near, feats_far = lax.optimization_barrier((near, feats_far))
    panels = {0: near, groups // 2: feats_far}
    for bit in reversed(bits_of(groups // 2)):
        for j in list(panels):
            panels[j ^ bit] = swap(panels[j], "blk", bit)

    half = groups // 2
    half_term = ((width // 2, width), BF16)
    tile = tiles.shape[-1]
    per = rows // tile
    live = jnp.arange(tiles.shape[3])[None, :] < tile_count[0, 0][:, None]
    live_tiles = jnp.where(live[..., None, None], tile_set, jnp.zeros((), BF16))
    spots = jnp.stack([place // per, place % per]) * tile
    local, near_term, send, *keep = call(
        functools.partial(adjacency_kernel, groups),
        [((rows, width), BF16), ((width, width), F32), ((half, width, rows), BF16)]
        + [((width, rows), BF16)] * half,
        [SMEM] * 2 + [VMEM] * (2 + groups),
        40 * MIB,
        [pltpu.VMEM((rows, groups * rows), BF16)],
    )(blk, spots, live_tiles, grad, *[panels[j] for j in range(groups)])
    got = swap(send, "blk", 1)

    kept, sent = call(
        halo_term_kernel,
        [half_term, half_term],
        [SMEM] + [VMEM] * 3,
        16 * MIB,
        [pltpu.VMEM((width, width), F32)],
        flops=2 * 10**10,
    )(blk, near_term, halo, outgoing)
    other = swap(sent, "blk", 1)
    inner = bits_of(groups)[1:]
    for bit in inner:
        later = [add(keep[j], got[j]) for j in range(1, len(keep), 2)]
        if bit == inner[0]:
            other, later[0] = lax.optimization_barrier((other, later[0]))
        if len(keep) == 2:
            third = swap(later[0], "blk", bit)
        else:
            keep = [add(keep[j], got[j]) for j in range(0, len(keep), 2)]
            got = swap(jnp.stack(later), "blk", bit)
    term = add(kept, other)
    bits = [("dom", bit) for bit in bits_of(peers)]
    bits = bits[1:] + bits[:1] + [("blk", bit) for bit in inner]
    fours = [bits[i : i + 2] for i in range(0, len(bits), 2)]
    for i, four in enumerate(fours):
        first, last = i == 0, i == len(fours) - 1
        if first:
            term, local = lax.optimization_barrier((term, local))
            (layer_out,) = call(
                output_kernel, [((rows, width), BF16)], [VMEM] * 5, 16 * MIB, flops=2 * 10**10
            )(local, halo, owner, edge, weight)
        if last:
            (feature_grad,) = call(
                backward_kernel, [((rows, width), BF16)], [SMEM] + [VMEM] * 6, 16 * MIB
            )(send_live, keep[0], got, third, halo, sends, weight)
        mate = fours[i ^ 1] if i ^ 1 < len(fours) and len(fours[i ^ 1]) == len(four) else four
        ways = [slice(0, 1), slice(1, 2), slice(0, 2)] if last else [slice(1, 2), slice(0, 2), slice(0, 1)]
        ways = ways if len(four) == 2 else [slice(0, 1)]
        others = [swap_bits(term, four[way], mate[way]) for way in ways]
        if first:
            others, layer_out = lax.optimization_barrier((others, layer_out))
        if last:
            others, feature_grad = lax.optimization_barrier((others, feature_grad))
        others = [others[ways.index(way)] for way in sorted(ways, key=str)]
        wide = [value.astype(F32) for value in (term, *others)]
        total = wide[0] + wide[1]
        if len(four) == 2:
            total += wide[2] + wide[3]
        term = total.astype(BF16)
    other = swap(term, "blk", 1)
    scale = float(groups * peers * rows) ** (-0.5)
    low = jnp.where(me % 2 == 0, term, other)
    high = jnp.where(me % 2 == 0, other, term)
    weight_grad = jnp.concatenate([low, high]).astype(F32) * scale
    return layer_out[None], feature_grad[None], weight_grad


def solution(mesh):
    return jax.shard_map(
        on_device,
        mesh=mesh,
        in_specs=(
            P("dom", "blk", None),
            P(),
            P("dom", "blk", None, None, None, None),
            P("dom", "blk", None, None),
            P("dom", "blk", None),
            P("dom", "blk", None, None),
            P("dom", "blk", None),
            P("dom", "blk", None, None),
            P("dom", "blk", None, None),
            P("dom", "blk", None),
        ),
        out_specs=(P("dom", "blk", None), P("dom", "blk", None), P()),
        check_vma=False,
    )
```

```python
import functools
import jax
import jax.numpy as jnp
from jax import lax
from jax.experimental import pallas as pl
from jax.experimental.pallas import tpu as pltpu
from jax.sharding import PartitionSpec as P

BF16 = jnp.bfloat16
F32 = jnp.float32
VMEM = pl.BlockSpec(memory_space=pltpu.VMEM)
SMEM = pl.BlockSpec(memory_space=pltpu.SMEM)
HBM = pl.BlockSpec(memory_space=pl.ANY)
MIB = 1 << 20


def swap(value, axis, bit):
    return lax.ppermute(value, axis, [(i, i ^ bit) for i in range(lax.axis_size(axis))])


def swap_bits(value, even, odd):
    groups, peers = lax.axis_size("blk"), lax.axis_size("dom")
    pairs = []
    for b in range(groups):
        bits = odd if b % 2 else even
        b_bits = sum(bit for axis, bit in bits if axis == "blk")
        d_bits = sum(bit for axis, bit in bits if axis == "dom")
        pairs += [(b * peers + d, (b ^ b_bits) * peers + (d ^ d_bits)) for d in range(peers)]
    return lax.ppermute(value, ("blk", "dom"), pairs)


def bits_of(size):
    return [1 << k for k in range(size.bit_length() - 1)]


def matmul(left, right, left_dim, right_dim):
    return lax.dot_general(
        left, right, (((left_dim,), (right_dim,)), ((), ())), preferred_element_type=F32
    )


def one_hot(rows, index):
    return lax.broadcasted_iota(jnp.int32, (rows, index.shape[1]), 0) == index


def flat(rows):
    return jnp.concatenate([rows[q : q + 1, :] for q in range(rows.shape[0])], axis=1)


def send_index_of(send_list, send_count):
    peers, slots = send_list.shape
    peer = lax.broadcasted_iota(jnp.int32, (peers, slots), 0)
    slot = lax.broadcasted_iota(jnp.int32, (peers, slots), 1)
    count = jnp.zeros((peers, slots), jnp.int32)
    for q in range(peers):
        count = jnp.where(peer == q, send_count[q], count)
    return flat(jnp.where(slot < count, send_list[...], -1))


def fetch(pairs, sems):
    copies = [pltpu.make_async_copy(src, dst, sems.at[i]) for i, (src, dst) in enumerate(pairs)]
    for copy in copies:
        copy.start()
    return copies


def halo_kernel(feats_in, grad_in, send_in, count_in, owner_in, edge_in, out, *scratch):
    feats, grad, send, count, owner, edge, sems = scratch
    sources = (feats_in, grad_in, send_in, count_in, owner_in, edge_in)
    for copy in fetch(list(zip(sources, scratch)), sems):
        copy.wait()
    rows, width = feats.shape
    peers, both, unused = out.shape
    slots = both // 2
    pick = one_hot(rows, send_index_of(send, count)).astype(BF16)
    sent = matmul(pick, feats[...], 0, 0)
    out[:, :slots, :] = sent.astype(BF16).reshape(peers, slots, width)
    back = matmul(weights_of(rows, owner, edge), grad[...], 0, 0)
    out[:, slots:, :] = back.astype(BF16).reshape(peers, slots, width)


def split_halves(blk, term, kept, sent):
    half = term.shape[0] // 2
    core = blk[0] % 2
    kept[...] = term[pl.ds(pl.multiple_of(core * half, half), half), :].astype(BF16)
    sent[...] = term[pl.ds(pl.multiple_of((1 - core) * half, half), half), :].astype(BF16)


def adjacency_kernel(groups, blk, spots, tiles, grad, *refs):
    panels, refs = refs[:groups], refs[groups:]
    (local, term, send, *keep), dense = refs[:-1], refs[-1]
    unused, slots, tile, unused = tiles.shape
    rows, width = grad.shape
    dense[...] = jnp.zeros_like(dense)
    for j in range(groups):
        c = blk[0] ^ j
        for t in range(slots):
            row = pl.multiple_of(spots[0, c, t], tile)
            column = pl.multiple_of(j * rows + spots[1, c, t], tile)
            dense[pl.ds(row, tile), pl.ds(column, tile)] = tiles[c, t]
    turned = grad[...].T
    for j in range(groups):
        part = matmul(turned, dense[:, j * rows : (j + 1) * rows], 1, 0).astype(BF16)
        if j % 2:
            send[j // 2] = part
        else:
            keep[j // 2][...] = part
    value = matmul(dense[:, :rows], panels[0][...], 1, 0)
    for j in range(1, groups):
        value += matmul(dense[:, j * rows : (j + 1) * rows], panels[j][...], 1, 0)
    rounded = value.astype(BF16)
    local[...] = rounded
    term[...] = matmul(rounded, grad[...], 0, 0)


def weights_of(rows, owner, edge):
    return jnp.where(one_hot(rows, flat(owner)), flat(edge), 0.0).astype(BF16)


def halo_sum(halo, owner, edge, rows):
    peers, both, width = halo.shape
    received = halo[:, : both // 2, :].reshape(-1, width)
    return matmul(weights_of(rows, owner, edge), received, 1, 0)


def halo_term_kernel(blk, near, halo, outgoing, kept, sent, term):
    peers, both, width = halo.shape
    received = halo[:, : both // 2, :].reshape(-1, width)
    weighted = outgoing[:, both // 2 :, :].reshape(-1, width)
    term[...] = near[...] + matmul(received, weighted, 0, 0)
    split_halves(blk, term, kept, sent)


def output_kernel(local, halo, owner, edge, weight, out):
    rows, width = out.shape
    total = local[...].astype(F32) + halo_sum(halo, owner, edge, rows)
    out[...] = matmul(total.astype(BF16), weight[...], 1, 0).astype(BF16)


def backward_kernel(send_count, first, others, third, halo, send_list, weight, out):
    rows, width = out.shape
    slots = halo.shape[1] // 2
    local = first[...].astype(F32) + others[0].astype(F32) + third[...].astype(F32)
    total = local.T + matmul(
        one_hot(rows, send_index_of(send_list, send_count)).astype(BF16),
        halo[:, slots:, :].reshape(-1, width),
        1,
        0,
    )
    out[...] = matmul(total.astype(BF16), weight[...], 1, 1).astype(BF16)


def call(kernel, outs, specs, limit, scratch=(), flops=1):
    return pl.pallas_call(
        kernel,
        out_shape=[jax.ShapeDtypeStruct(shape, dtype) for shape, dtype in outs],
        in_specs=specs,
        out_specs=[VMEM] * len(outs),
        scratch_shapes=list(scratch),
        cost_estimate=pl.CostEstimate(flops=flops, bytes_accessed=1, transcendentals=0),
        compiler_params=pltpu.CompilerParams(vmem_limit_bytes=limit),
    )


def add(*values):
    return sum(value.astype(F32) for value in values).astype(BF16)


def on_device(
    features,
    weight,
    tiles,
    tile_pos,
    tile_count,
    send_list,
    send_count,
    owner_map,
    halo_weight,
    cotangent,
):
    groups, peers = lax.axis_size("blk"), lax.axis_size("dom")
    feats, grad = features[0], cotangent[0]
    rows, width = feats.shape
    slots = send_list.shape[-1]
    links = peers * slots
    me = lax.axis_index("blk").astype(jnp.int32)
    blk = me.reshape(1)
    sends, send_live = send_list[0, 0], send_count[0, 0]
    owner, edge = owner_map[0, 0], halo_weight[0, 0]

    feats_far = swap(feats, "blk", groups // 2)
    (outgoing,) = call(
        halo_kernel,
        [((peers, 2 * slots, width), BF16)],
        [HBM] * 6,
        64 * MIB,
        [
            pltpu.VMEM((rows, width), BF16),
            pltpu.VMEM((rows, width), BF16),
            pltpu.VMEM((peers, slots), jnp.int32),
            pltpu.SMEM((peers,), jnp.int32),
            pltpu.VMEM((peers, slots), jnp.int32),
            pltpu.VMEM((peers, slots), F32),
            pltpu.SemaphoreType.DMA((6,)),
        ],
    )(feats, grad, sends, send_live, owner, edge)
    outgoing, near, tile_set, place = lax.optimization_barrier(
        (outgoing, feats, tiles[0, 0], tile_pos[0, 0])
    )
    halo = lax.all_to_all(outgoing, "dom", split_axis=0, concat_axis=0, tiled=True)

    near, feats_far = lax.optimization_barrier((near, feats_far))
    panels = {0: near, groups // 2: feats_far}
    for bit in reversed(bits_of(groups // 2)):
        for j in list(panels):
            panels[j ^ bit] = swap(panels[j], "blk", bit)

    half = groups // 2
    half_term = ((width // 2, width), BF16)
    tile = tiles.shape[-1]
    per = rows // tile
    live = jnp.arange(tiles.shape[3])[None, :] < tile_count[0, 0][:, None]
    live_tiles = jnp.where(live[..., None, None], tile_set, jnp.zeros((), BF16))
    spots = jnp.stack([place // per, place % per]) * tile
    local, near_term, send, *keep = call(
        functools.partial(adjacency_kernel, groups),
        [((rows, width), BF16), ((width, width), F32), ((half, width, rows), BF16)]
        + [((width, rows), BF16)] * half,
        [SMEM] * 2 + [VMEM] * (2 + groups),
        40 * MIB,
        [pltpu.VMEM((rows, groups * rows), BF16)],
    )(blk, spots, live_tiles, grad, *[panels[j] for j in range(groups)])
    got = swap(send, "blk", 1)

    kept, sent = call(
        halo_term_kernel,
        [half_term, half_term],
        [SMEM] + [VMEM] * 3,
        16 * MIB,
        [pltpu.VMEM((width, width), F32)],
        flops=2 * 10**10,
    )(blk, near_term, halo, outgoing)
    other = swap(sent, "blk", 1)
    inner = bits_of(groups)[1:]
    for bit in inner:
        later = [add(keep[j], got[j]) for j in range(1, len(keep), 2)]
        if bit == inner[0]:
            other, later[0] = lax.optimization_barrier((other, later[0]))
        if len(keep) == 2:
            third = swap(later[0], "blk", bit)
        else:
            keep = [add(keep[j], got[j]) for j in range(0, len(keep), 2)]
            got = swap(jnp.stack(later), "blk", bit)
    term = add(kept, other)
    bits = [("dom", bit) for bit in bits_of(peers)]
    bits = bits[1:] + bits[:1] + [("blk", bit) for bit in inner]
    fours = [bits[i : i + 2] for i in range(0, len(bits), 2)]
    for i, four in enumerate(fours):
        first, last = i == 0, i == len(fours) - 1
        if first:
            term, local = lax.optimization_barrier((term, local))
            (layer_out,) = call(
                output_kernel, [((rows, width), BF16)], [VMEM] * 5, 16 * MIB, flops=2 * 10**10
            )(local, halo, owner, edge, weight)
        if last:
            (feature_grad,) = call(
                backward_kernel, [((rows, width), BF16)], [SMEM] + [VMEM] * 6, 16 * MIB
            )(send_live, keep[0], got, third, halo, sends, weight)
        mate = fours[i ^ 1] if i ^ 1 < len(fours) and len(fours[i ^ 1]) == len(four) else four
        ways = [slice(0, 1), slice(1, 2), slice(0, 2)] if last else [slice(0, 2), slice(0, 1), slice(1, 2)]
        ways = ways if len(four) == 2 else [slice(0, 1)]
        others = [swap_bits(term, four[way], mate[way]) for way in ways]
        if first:
            others, layer_out = lax.optimization_barrier((others, layer_out))
        if last:
            others, feature_grad = lax.optimization_barrier((others, feature_grad))
        others = [others[ways.index(way)] for way in sorted(ways, key=str)]
        wide = [value.astype(F32) for value in (term, *others)]
        total = wide[0] + wide[1]
        if len(four) == 2:
            total += wide[2] + wide[3]
        term = total.astype(BF16)
    other = swap(term, "blk", 1)
    scale = float(groups * peers * rows) ** (-0.5)
    low = jnp.where(me % 2 == 0, term, other)
    high = jnp.where(me % 2 == 0, other, term)
    weight_grad = jnp.concatenate([low, high]).astype(F32) * scale
    return layer_out[None], feature_grad[None], weight_grad


def solution(mesh):
    return jax.shard_map(
        on_device,
        mesh=mesh,
        in_specs=(
            P("dom", "blk", None),
            P(),
            P("dom", "blk", None, None, None, None),
            P("dom", "blk", None, None),
            P("dom", "blk", None),
            P("dom", "blk", None, None),
            P("dom", "blk", None),
            P("dom", "blk", None, None),
            P("dom", "blk", None, None),
            P("dom", "blk", None),
        ),
        out_specs=(P("dom", "blk", None), P("dom", "blk", None), P()),
        check_vma=False,
    )
```

```python
import functools
import jax
import jax.numpy as jnp
from jax import lax
from jax.experimental import pallas as pl
from jax.experimental.pallas import tpu as pltpu
from jax.sharding import PartitionSpec as P

BF16 = jnp.bfloat16
F32 = jnp.float32
VMEM = pl.BlockSpec(memory_space=pltpu.VMEM)
SMEM = pl.BlockSpec(memory_space=pltpu.SMEM)
HBM = pl.BlockSpec(memory_space=pl.ANY)
MIB = 1 << 20


def swap(value, axis, bit):
    return lax.ppermute(value, axis, [(i, i ^ bit) for i in range(lax.axis_size(axis))])


def swap_bits(value, even, odd):
    groups, peers = lax.axis_size("blk"), lax.axis_size("dom")
    pairs = []
    for b in range(groups):
        bits = odd if b % 2 else even
        b_bits = sum(bit for axis, bit in bits if axis == "blk")
        d_bits = sum(bit for axis, bit in bits if axis == "dom")
        pairs += [(b * peers + d, (b ^ b_bits) * peers + (d ^ d_bits)) for d in range(peers)]
    return lax.ppermute(value, ("blk", "dom"), pairs)


def bits_of(size):
    return [1 << k for k in range(size.bit_length() - 1)]


def matmul(left, right, left_dim, right_dim):
    return lax.dot_general(
        left, right, (((left_dim,), (right_dim,)), ((), ())), preferred_element_type=F32
    )


def one_hot(rows, index):
    return lax.broadcasted_iota(jnp.int32, (rows, index.shape[1]), 0) == index


def flat(rows):
    return jnp.concatenate([rows[q : q + 1, :] for q in range(rows.shape[0])], axis=1)


def send_index_of(send_list, send_count):
    peers, slots = send_list.shape
    peer = lax.broadcasted_iota(jnp.int32, (peers, slots), 0)
    slot = lax.broadcasted_iota(jnp.int32, (peers, slots), 1)
    count = jnp.zeros((peers, slots), jnp.int32)
    for q in range(peers):
        count = jnp.where(peer == q, send_count[q], count)
    return flat(jnp.where(slot < count, send_list[...], -1))


def fetch(pairs, sems):
    copies = [pltpu.make_async_copy(src, dst, sems.at[i]) for i, (src, dst) in enumerate(pairs)]
    for copy in copies:
        copy.start()
    return copies


def halo_kernel(feats_in, grad_in, send_in, count_in, owner_in, edge_in, out, *scratch):
    feats, grad, send, count, owner, edge, sems = scratch
    sources = (feats_in, grad_in, send_in, count_in, owner_in, edge_in)
    for copy in fetch(list(zip(sources, scratch)), sems):
        copy.wait()
    rows, width = feats.shape
    peers, both, unused = out.shape
    slots = both // 2
    pick = one_hot(rows, send_index_of(send, count)).astype(BF16)
    sent = matmul(pick, feats[...], 0, 0)
    out[:, :slots, :] = sent.astype(BF16).reshape(peers, slots, width)
    back = matmul(weights_of(rows, owner, edge), grad[...], 0, 0)
    out[:, slots:, :] = back.astype(BF16).reshape(peers, slots, width)


def adjacency_kernel(groups, blk, spots, tiles, grad, *refs):
    panels, refs = refs[:groups], refs[groups:]
    (local, term, send, *keep), dense = refs[:-1], refs[-1]
    unused, slots, tile, unused = tiles.shape
    rows, width = grad.shape
    dense[...] = jnp.zeros_like(dense)
    for j in range(groups):
        c = blk[0] ^ j
        for t in range(slots):
            row = pl.multiple_of(spots[0, c, t], tile)
            column = pl.multiple_of(j * rows + spots[1, c, t], tile)
            dense[pl.ds(row, tile), pl.ds(column, tile)] = tiles[c, t]
    turned = grad[...].T
    for j in range(groups):
        part = matmul(turned, dense[:, j * rows : (j + 1) * rows], 1, 0).astype(BF16)
        if j % 2:
            send[j // 2] = part
        else:
            keep[j // 2][...] = part
    value = matmul(dense[:, :rows], panels[0][...], 1, 0)
    for j in range(1, groups):
        value += matmul(dense[:, j * rows : (j + 1) * rows], panels[j][...], 1, 0)
    rounded = value.astype(BF16)
    local[...] = rounded
    term[...] = matmul(rounded, grad[...], 0, 0)


def weights_of(rows, owner, edge):
    return jnp.where(one_hot(rows, flat(owner)), flat(edge), 0.0).astype(BF16)


def halo_sum(halo, owner, edge, rows):
    peers, both, width = halo.shape
    received = halo[:, : both // 2, :].reshape(-1, width)
    return matmul(weights_of(rows, owner, edge), received, 1, 0)


def halo_term_kernel(blk, near, halo, outgoing, kept, sent):
    peers, both, width = halo.shape
    received = halo[:, : both // 2, :].reshape(-1, width)
    weighted = outgoing[:, both // 2 :, :].reshape(-1, width)
    product = near[...] + matmul(received, weighted, 0, 0)
    low, high = product[: width // 2].astype(BF16), product[width // 2 :].astype(BF16)
    first = blk[0] % 2 == 0
    kept[...] = jnp.where(first, low, high)
    sent[...] = jnp.where(first, high, low)


def output_kernel(local, halo, owner, edge, weight, out):
    rows, width = out.shape
    total = local[...].astype(F32) + halo_sum(halo, owner, edge, rows)
    out[...] = matmul(total.astype(BF16), weight[...], 1, 0).astype(BF16)


def backward_kernel(send_count, first, others, third, halo, send_list, weight, out):
    rows, width = out.shape
    slots = halo.shape[1] // 2
    local = first[...].astype(F32) + others[0].astype(F32) + third[...].astype(F32)
    total = local.T + matmul(
        one_hot(rows, send_index_of(send_list, send_count)).astype(BF16),
        halo[:, slots:, :].reshape(-1, width),
        1,
        0,
    )
    out[...] = matmul(total.astype(BF16), weight[...], 1, 1).astype(BF16)


def call(kernel, outs, specs, limit, scratch=(), flops=1):
    return pl.pallas_call(
        kernel,
        out_shape=[jax.ShapeDtypeStruct(shape, dtype) for shape, dtype in outs],
        in_specs=specs,
        out_specs=[VMEM] * len(outs),
        scratch_shapes=list(scratch),
        cost_estimate=pl.CostEstimate(flops=flops, bytes_accessed=1, transcendentals=0),
        compiler_params=pltpu.CompilerParams(vmem_limit_bytes=limit),
    )


def add(*values):
    return sum(value.astype(F32) for value in values).astype(BF16)


def on_device(
    features,
    weight,
    tiles,
    tile_pos,
    tile_count,
    send_list,
    send_count,
    owner_map,
    halo_weight,
    cotangent,
):
    groups, peers = lax.axis_size("blk"), lax.axis_size("dom")
    feats, grad = features[0], cotangent[0]
    rows, width = feats.shape
    slots = send_list.shape[-1]
    links = peers * slots
    me = lax.axis_index("blk").astype(jnp.int32)
    blk = me.reshape(1)
    sends, send_live = send_list[0, 0], send_count[0, 0]
    owner, edge = owner_map[0, 0], halo_weight[0, 0]

    feats_far = swap(feats, "blk", groups // 2)
    (outgoing,) = call(
        halo_kernel,
        [((peers, 2 * slots, width), BF16)],
        [HBM] * 6,
        64 * MIB,
        [
            pltpu.VMEM((rows, width), BF16),
            pltpu.VMEM((rows, width), BF16),
            pltpu.VMEM((peers, slots), jnp.int32),
            pltpu.SMEM((peers,), jnp.int32),
            pltpu.VMEM((peers, slots), jnp.int32),
            pltpu.VMEM((peers, slots), F32),
            pltpu.SemaphoreType.DMA((6,)),
        ],
    )(feats, grad, sends, send_live, owner, edge)
    outgoing, near, tile_set, place = lax.optimization_barrier(
        (outgoing, feats, tiles[0, 0], tile_pos[0, 0])
    )
    halo = lax.all_to_all(outgoing, "dom", split_axis=0, concat_axis=0, tiled=True)

    near, feats_far = lax.optimization_barrier((near, feats_far))
    panels = {0: near, groups // 2: feats_far}
    for bit in reversed(bits_of(groups // 2)):
        for j in list(panels):
            panels[j ^ bit] = swap(panels[j], "blk", bit)

    half = groups // 2
    half_term = ((width // 2, width), BF16)
    tile = tiles.shape[-1]
    per = rows // tile
    live = jnp.arange(tiles.shape[3])[None, :] < tile_count[0, 0][:, None]
    live_tiles = jnp.where(live[..., None, None], tile_set, jnp.zeros((), BF16))
    spots = jnp.stack([place // per, place % per]) * tile
    local, near_term, send, *keep = call(
        functools.partial(adjacency_kernel, groups),
        [((rows, width), BF16), ((width, width), F32), ((half, width, rows), BF16)]
        + [((width, rows), BF16)] * half,
        [SMEM] * 2 + [VMEM] * (2 + groups),
        40 * MIB,
        [pltpu.VMEM((rows, groups * rows), BF16)],
    )(blk, spots, live_tiles, grad, *[panels[j] for j in range(groups)])
    got = swap(send, "blk", 1)

    kept, sent = call(
        halo_term_kernel,
        [half_term, half_term],
        [SMEM] + [VMEM] * 3,
        16 * MIB,
        flops=2 * 10**10,
    )(blk, near_term, halo, outgoing)
    other = swap(sent, "blk", 1)
    inner = bits_of(groups)[1:]
    for bit in inner:
        later = [add(keep[j], got[j]) for j in range(1, len(keep), 2)]
        if bit == inner[0]:
            other, later[0] = lax.optimization_barrier((other, later[0]))
        if len(keep) == 2:
            third = swap(later[0], "blk", bit)
        else:
            keep = [add(keep[j], got[j]) for j in range(0, len(keep), 2)]
            got = swap(jnp.stack(later), "blk", bit)
    term = add(kept, other)
    bits = [("dom", bit) for bit in bits_of(peers)]
    bits = bits[1:] + bits[:1] + [("blk", bit) for bit in inner]
    fours = [bits[i : i + 2] for i in range(0, len(bits), 2)]
    for i, four in enumerate(fours):
        first, last = i == 0, i == len(fours) - 1
        if first:
            term, local = lax.optimization_barrier((term, local))
            (layer_out,) = call(
                output_kernel, [((rows, width), BF16)], [VMEM] * 5, 16 * MIB, flops=2 * 10**10
            )(local, halo, owner, edge, weight)
        if last:
            (feature_grad,) = call(
                backward_kernel, [((rows, width), BF16)], [SMEM] + [VMEM] * 6, 16 * MIB
            )(send_live, keep[0], got, third, halo, sends, weight)
        mate = fours[i ^ 1] if i ^ 1 < len(fours) and len(fours[i ^ 1]) == len(four) else four
        ways = [slice(0, 1), slice(1, 2), slice(0, 2)] if last else [slice(0, 2), slice(0, 1), slice(1, 2)]
        ways = ways if len(four) == 2 else [slice(0, 1)]
        others = [swap_bits(term, four[way], mate[way]) for way in ways]
        if first:
            others, layer_out = lax.optimization_barrier((others, layer_out))
        if last:
            others, feature_grad = lax.optimization_barrier((others, feature_grad))
        others = [others[ways.index(way)] for way in sorted(ways, key=str)]
        wide = [value.astype(F32) for value in (term, *others)]
        total = wide[0] + wide[1]
        if len(four) == 2:
            total += wide[2] + wide[3]
        term = total.astype(BF16)
    other = swap(term, "blk", 1)
    scale = float(groups * peers * rows) ** (-0.5)
    low = jnp.where(me % 2 == 0, term, other)
    high = jnp.where(me % 2 == 0, other, term)
    weight_grad = jnp.concatenate([low, high]).astype(F32) * scale
    return layer_out[None], feature_grad[None], weight_grad


def solution(mesh):
    return jax.shard_map(
        on_device,
        mesh=mesh,
        in_specs=(
            P("dom", "blk", None),
            P(),
            P("dom", "blk", None, None, None, None),
            P("dom", "blk", None, None),
            P("dom", "blk", None),
            P("dom", "blk", None, None),
            P("dom", "blk", None),
            P("dom", "blk", None, None),
            P("dom", "blk", None, None),
            P("dom", "blk", None),
        ),
        out_specs=(P("dom", "blk", None), P("dom", "blk", None), P()),
        check_vma=False,
    )
```
